32 devices in a mesh: ctx: 8 (over z, x), kvh: 4 (over y, core).
Axes of the slice: x: 2, y: 2, z: 4, core: 2. Of those that a mesh axis runs over, the one named last changes fastest.
Arguments:
- queries: bfloat16 [1024, 4096], P('ctx', 'kvh'), may hold values from -6 to 6
- keys: bfloat16 [1024, 512], P('ctx', 'kvh'), may hold values from -6 to 6
- values: bfloat16 [1024, 512], P('ctx', 'kvh'), may hold values from -6 to 6
- upstream: bfloat16 [1024, 4096], P('ctx', 'kvh'), may hold values from -6 to 6
- selected: int32 [8, 8], P('ctx'), may hold values from -1 to 14, as said below
- counts: int32 [8], P('ctx'), may hold values from 1 to 4, as said below
Outputs:
- attention: bfloat16 [1024, 4096], P('ctx', 'kvh')
- grad_queries: bfloat16 [1024, 4096], P(('ctx', 'kvh'))
- grad_keys: float32 [1024, 512], P('ctx', 'kvh')
- grad_values: float32 [1024, 512], P('ctx', 'kvh')
The draws below stay inside these ranges and needn't reach their ends.
Inputs may be any that keep to these rules, and one draw needn't show every extreme that they name: `selected`: slot 0 of query block b is key block 2 b. Slot j >= 1 names one of the 2 key blocks held by the index of ctx that lies 2 ** (j - 1) below the index holding query block b, or is -1 where that index would be negative. counts[b] is at most 1 plus the number of non-negative remote slots of query block b; all slots j < counts[b] are non-negative.
All inputs are finite; a program needn't handle non-finite values.
Results may differ from the reference program's by a relative error of at most 0.04.
Values may be sent and summed in bfloat16 or wider, within the bound.
A program may use at most 64 MiB of HBM per device.

```python
import math
import jax
import jax.numpy as jnp
from jax import lax

HD = 128
GROUP = 8
KVH = 4
KBLK = 64
QBLK = 128
SLOTS = 8
QB_DEV = 1
KB_DEV = 2
NQB = 8
TOKENS = 1024


def selection_tables(key):
    block_ids = jnp.arange(NQB, dtype=jnp.int32)
    owner_dev = block_ids // QB_DEV
    distances = jnp.left_shift(jnp.int32(1), jnp.arange(SLOTS - 1, dtype=jnp.int32))
    source_dev = owner_dev[:, None] - distances[None, :]
    usable = source_dev >= 0
    available = jnp.sum(usable.astype(jnp.int32), axis=1)
    raw_count = jax.random.randint(jax.random.fold_in(key, 11), (NQB,), 1, SLOTS + 1)
    live_count = jnp.minimum(raw_count, 1 + available)
    live_count = jnp.where(block_ids == NQB - 1, 1 + available, live_count).astype(jnp.int32)
    inner = jax.random.randint(jax.random.fold_in(key, 13), (NQB, SLOTS - 1), 0, KB_DEV)
    remote = jnp.where(usable, source_dev * KB_DEV + inner, -1).astype(jnp.int32)
    chosen = jnp.concatenate([(2 * block_ids)[:, None], remote], axis=1).astype(jnp.int32)
    return (chosen, live_count)


def draw_selected(key, part):
    return selection_tables(key)[0]


def draw_counts(key, part):
    return selection_tables(key)[1]


def draw_queries(key, part):
    shape = (TOKENS, KVH * GROUP * HD)
    bulk = jnp.clip(jax.random.normal(jax.random.fold_in(key, 41), shape, jnp.float32), -6.0, 6.0)
    return bulk.astype(jnp.bfloat16)


def draw_keys(key, part):
    shape = (TOKENS, KVH * HD)
    bulk = jnp.clip(jax.random.normal(jax.random.fold_in(key, 42), shape, jnp.float32), -6.0, 6.0)
    return bulk.astype(jnp.bfloat16)


def block_scale(stream_key, extent, cuts, low, largest):
    factor_of = 1.0
    for axis_at, blocks in cuts:
        draws = jax.random.uniform(jax.random.fold_in(jax.random.fold_in(stream_key, 6), axis_at), (blocks,), jnp.float32, low / len(cuts), largest / len(cuts))
        factor_of = factor_of * jnp.repeat(jnp.exp(draws), extent[axis_at] // blocks).reshape((-1,) + (1,) * (len(extent) - 1 - axis_at))
    return factor_of


def noise(stream_key, extent, scale, limit, pieces=(), held_as=jnp.bfloat16):
    result = scale * jax.random.normal(stream_key, extent, jnp.float32)
    if pieces:
        result = result * block_scale(stream_key, extent, pieces, -0.22, 0.18)
    return jnp.clip(result, -limit, limit).astype(held_as)


def setup_inputs(seed: int = 0) -> dict:
    streams_of = jax.random.split(jax.random.key(seed), 7)
    return {
        "queries": draw_queries(jax.random.fold_in(streams_of[6], 71), 0),
        "keys": draw_keys(jax.random.fold_in(streams_of[6], 71), 0),
        "values": noise(streams_of[2], (TOKENS, KVH * HD), 1.0, 6.0, ((0, 8), (1, 4))),
        "upstream": noise(streams_of[3], (TOKENS, KVH * GROUP * HD), 1.0, 6.0, ((0, 8), (1, 4))),
        "selected": draw_selected(jax.random.fold_in(streams_of[6], 71), 0),
        "counts": draw_counts(jax.random.fold_in(streams_of[6], 71), 0),
    }


def block_pass(query_heads, key_rows, value_rows, grad_heads, visible):
    score_scale = 1.0 / math.sqrt(HD)
    scores = jnp.einsum('ihd,sd->his', query_heads.astype(jnp.float32), key_rows.astype(jnp.float32)) * score_scale
    scores = jnp.where(visible[None], scores, jnp.float32(-1e+30))
    peak = lax.optimization_barrier(jnp.max(scores, axis=-1, keepdims=True))
    expon = jnp.exp(scores - peak)
    prob = expon / lax.optimization_barrier(jnp.sum(expon, axis=-1, keepdims=True))
    prob_half = prob.astype(jnp.bfloat16)
    attended = jnp.einsum('his,sd->ihd', prob_half.astype(jnp.float32), value_rows.astype(jnp.float32)).astype(jnp.bfloat16)
    grad_probs = jnp.einsum('ihd,sd->his', grad_heads.astype(jnp.float32), value_rows.astype(jnp.float32))
    row_term = lax.optimization_barrier(jnp.sum(grad_heads.astype(jnp.float32) * attended.astype(jnp.float32), axis=-1))
    grad_scores = (prob * (grad_probs - jnp.transpose(row_term)[:, :, None]) * score_scale).astype(jnp.bfloat16)
    grad_query = jnp.einsum('his,sd->ihd', grad_scores.astype(jnp.float32), key_rows.astype(jnp.float32)).astype(jnp.bfloat16)
    key_term = jnp.einsum('his,ihd->sd', grad_scores.astype(jnp.float32), query_heads.astype(jnp.float32))
    value_term = jnp.einsum('his,ihd->sd', prob_half.astype(jnp.float32), grad_heads.astype(jnp.float32))
    return (attended, grad_query, key_term, value_term)

def reference(queries, keys, values, upstream, selected, counts):
    width = GROUP * HD
    slot_index = jnp.arange(SLOTS * KBLK, dtype=jnp.int32) // KBLK
    offsets = jnp.arange(SLOTS * KBLK, dtype=jnp.int32) % KBLK

    def one_block(running, block_id):
        key_acc, value_acc = running
        first_row = (block_id * QBLK).astype(jnp.int32)
        query_rows = lax.dynamic_slice_in_dim(queries, first_row, QBLK, 0)
        grad_rows = lax.dynamic_slice_in_dim(upstream, first_row, QBLK, 0)
        chosen = selected[block_id]
        live_count = counts[block_id]
        key_pos = chosen[slot_index] * KBLK + offsets
        token_rows = jnp.clip(key_pos, 0, TOKENS - 1)
        query_pos = first_row + jnp.arange(QBLK, dtype=jnp.int32)
        visible = (slot_index < live_count)[None, :] & (key_pos[None, :] <= query_pos[:, None])
        outputs = []
        grads = []
        for group in range(KVH):
            query_heads = query_rows[:, group * width:(group + 1) * width].reshape(QBLK, GROUP, HD)
            grad_heads = grad_rows[:, group * width:(group + 1) * width].reshape(QBLK, GROUP, HD)
            key_rows = keys[token_rows, group * HD:(group + 1) * HD]
            value_rows = values[token_rows, group * HD:(group + 1) * HD]
            attended, grad_query, key_term, value_term = block_pass(query_heads, key_rows, value_rows, grad_heads, visible)
            outputs.append(attended.reshape(QBLK, width))
            grads.append(grad_query.reshape(QBLK, width))
            key_acc = key_acc.at[token_rows, group * HD:(group + 1) * HD].add(key_term)
            value_acc = value_acc.at[token_rows, group * HD:(group + 1) * HD].add(value_term)
        return ((key_acc, value_acc), (jnp.concatenate(outputs, axis=1), jnp.concatenate(grads, axis=1)))
    start_acc = (jnp.zeros((TOKENS, KVH * HD), jnp.float32), jnp.zeros((TOKENS, KVH * HD), jnp.float32))
    (key_acc, value_acc), (attn_blocks, grad_blocks) = lax.scan(one_block, start_acc, jnp.arange(NQB, dtype=jnp.int32))
    attention = attn_blocks.reshape(TOKENS, KVH * width)
    grad_queries = grad_blocks.reshape(TOKENS, KVH * width)
    return (attention, grad_queries, key_acc, value_acc)
```

```python
import functools
import math

import jax
import jax.numpy as jnp
from jax import lax
from jax.experimental import pallas as pl
from jax.experimental.pallas import tpu as pltpu
from jax.sharding import PartitionSpec as P

HD = 128
GROUP = 8
KBLK = 64
QBLK = 128
SLOTS = 8
PAIR = 2

MESH = pl.DeviceIdType.MESH
LOG2E = math.log2(math.e)
NT = (((1,), (1,)), ((), ()))
NN = (((1,), (0,)), ((), ()))


def dot(a, b, dims):
    return lax.dot_general(a, b, dims, preferred_element_type=jnp.float32)


def kernel(
    ctx_count,
    kvh_count,
    distances,
    sel_ref,
    cnt_ref,
    q_hbm,
    k_hbm,
    v_hbm,
    u_hbm,
    att_hbm,
    gq_hbm,
    gk_hbm,
    gv_hbm,
    q_v,
    u_v,
    k_own,
    v_own,
    k_in,
    v_in,
    sel_out,
    sel_in,
    keys,
    vals,
    att_v,
    gq_v,
    terms,
    terms_out,
    terms_in,
    total,
    load_sem,
    store_sem,
    kv_send,
    kv_recv,
    sel_send,
    sel_recv,
    term_send,
    term_recv,
    gq_send,
    gq_recv,
    gq_local,
):
    score_scale = 1.0 / math.sqrt(HD)
    me = lax.axis_index("ctx")
    head = lax.axis_index("kvh")
    slots = 1 + len(distances)
    part = QBLK // kvh_count
    width = GROUP * HD
    chunks = GROUP // PAIR

    loads = [
        pltpu.make_async_copy(src, dst, load_sem.at[i])
        for i, (src, dst) in enumerate(
            [(k_hbm, k_own), (v_hbm, v_own), (q_hbm, q_v), (u_hbm, u_v)]
        )
    ]
    for copy in loads:
        copy.start()

    barrier = pltpu.get_barrier_semaphore()
    for r in range(1, kvh_count):
        peer = lax.rem(head + r, kvh_count)
        pl.semaphore_signal(barrier, inc=1, device_id={"kvh": peer}, device_id_type=MESH)
    for d in distances:

        @pl.when(me + d < ctx_count)
        def _():
            pl.semaphore_signal(barrier, inc=1, device_id={"ctx": me + d}, device_id_type=MESH)

        @pl.when(me - d >= 0)
        def _():
            pl.semaphore_signal(barrier, inc=1, device_id={"ctx": me - d}, device_id_type=MESH)

    for j, d in enumerate(distances):
        sel_out[j] = jnp.full((8, HD), sel_ref[0, j + 1] - 2 * (me - d), jnp.int32)

    partners = kvh_count - 1
    for d in distances:
        partners += 1 - (me + d) // ctx_count + (me - d + ctx_count) // ctx_count
    pl.semaphore_wait(barrier, partners)

    def remote(src, dst, send, recv, **where):
        return pltpu.make_async_remote_copy(
            src_ref=src, dst_ref=dst, send_sem=send, recv_sem=recv,
            device_id=where, device_id_type=MESH,
        )

    def k_copy(j, d):
        return remote(k_hbm, k_in.at[j], kv_send.at[0, j], kv_recv.at[0, j], ctx=me + d)

    def v_copy(j, d):
        return remote(v_hbm, v_in.at[j], kv_send.at[1, j], kv_recv.at[1, j], ctx=me + d)

    def sel_copy(j, d):
        return remote(sel_out.at[j], sel_in.at[j], sel_send.at[j], sel_recv.at[j], ctx=me - d)

    def term_copy(j, d):
        return remote(terms_out.at[j], terms_in.at[j], term_send.at[j], term_recv.at[j], ctx=me - d)

    def gq_copy(c, r):
        cols = PAIR * HD
        peer = lax.rem(head + r, kvh_count)
        return remote(
            gq_v.at[pl.ds(pl.multiple_of(peer * part, part), part), pl.ds(c * cols, cols)],
            gq_hbm.at[:, pl.ds(pl.multiple_of(head * width + c * cols, cols), cols)],
            gq_send.at[c, r - 1],
            gq_recv.at[c, r - 1],
            kvh=peer,
        )

    by_far = list(enumerate(distances))[::-1]
    for make in (k_copy, v_copy):
        for j, d in by_far:

            @pl.when(me + d < ctx_count)
            def _(make=make, j=j, d=d):
                make(j, d).start()

    for j, d in by_far:

        @pl.when(me - d >= 0)
        def _(j=j, d=d):
            sel_copy(j, d).start()

    for copy in loads:
        copy.wait()
    keys[0:KBLK] = k_own[0:KBLK]
    vals[0:KBLK] = v_own[0:KBLK]
    count = cnt_ref[0]
    for make, arrived, chosen in ((k_copy, k_in, keys), (v_copy, v_in, vals)):
        for j, d in enumerate(distances):

            @pl.when(me - d >= 0)
            def _(make=make, j=j, d=d):
                make(j, d).wait_recv()

            live = jnp.full((KBLK, HD), count > j + 1)
            upper = jnp.full((KBLK, HD), sel_ref[0, j + 1] - 2 * (me - d) > 0)
            lo = arrived[j, 0:KBLK].astype(jnp.float32)
            hi = arrived[j, KBLK : 2 * KBLK].astype(jnp.float32)
            rows = jnp.where(live, jnp.where(upper, hi, lo), 0.0)
            chosen[(j + 1) * KBLK : (j + 2) * KBLK] = rows.astype(jnp.bfloat16)

    k_all = keys[...]
    v_all = vals[...]
    k_t = k_all.astype(jnp.float32).T.astype(jnp.bfloat16)
    v_t = v_all.astype(jnp.float32).T.astype(jnp.bfloat16)

    lanes = PAIR * QBLK
    key_at = lax.broadcasted_iota(jnp.int32, (KBLK, lanes), 0)
    query_at = lax.rem(lax.broadcasted_iota(jnp.int32, (KBLK, lanes), 1), QBLK)
    causal = key_at <= query_at
    hidden = [jnp.full((KBLK, lanes), count <= j) for j in range(1, slots)]

    for c in range(chunks):
        heads = [slice((c * PAIR + i) * HD, (c * PAIR + i + 1) * HD) for i in range(PAIR)]
        q = jnp.concatenate([q_v[:, h] for h in heads], axis=0)
        u = jnp.concatenate([u_v[:, h] for h in heads], axis=0)
        s = dot(k_all, q, NT)
        s = jnp.concatenate(
            [jnp.where(causal, s[0:KBLK], -1e30)]
            + [
                jnp.where(hidden[j - 1], -1e30, s[j * KBLK : (j + 1) * KBLK])
                for j in range(1, slots)
            ],
            axis=0,
        )
        peak = jnp.max(s, axis=0, keepdims=True)
        e = jnp.exp2((s - peak) * (score_scale * LOG2E))
        p = e * (1.0 / jnp.sum(e, axis=0, keepdims=True))
        p_half = p.astype(jnp.bfloat16)
        dp = dot(v_all, u, NT)
        row_term = jnp.sum(p * dp, axis=0, keepdims=True)
        ds = (p * (dp - row_term)).astype(jnp.bfloat16)
        gq_t = dot(k_t, ds, NN) * score_scale
        att_t = dot(v_t, p_half, NN)
        for i, h in enumerate(heads):
            gq_v[:, h] = gq_t[:, i * QBLK : (i + 1) * QBLK].T.astype(jnp.bfloat16)
            att_v[:, h] = att_t[:, i * QBLK : (i + 1) * QBLK].T.astype(jnp.bfloat16)
        for r in range(1, kvh_count):
            gq_copy(c, r).start()
        k_term = dot(ds, q, NN) * score_scale
        v_term = dot(p_half, u, NN)
        if c == 0:
            terms[0] = k_term
            terms[1] = v_term
        else:
            terms[0] += k_term
            terms[1] += v_term

    for j, d in by_far:
        rows = slice((j + 1) * KBLK, (j + 2) * KBLK)
        terms_out[j, 0:KBLK] = terms[0, rows].astype(jnp.bfloat16)
        terms_out[j, KBLK : 2 * KBLK] = terms[1, rows].astype(jnp.bfloat16)

        @pl.when(me - d >= 0)
        def _(j=j, d=d):
            term_copy(j, d).start()

    att_store = pltpu.make_async_copy(att_v, att_hbm, store_sem.at[0])
    att_store.start()
    gq_store = pltpu.make_async_copy(
        gq_v.at[pl.ds(pl.multiple_of(head * part, part), part), :],
        gq_hbm.at[:, pl.ds(pl.multiple_of(head * width, width), width)],
        gq_local,
    )
    gq_store.start()

    for i in range(2):
        total[i, 0:KBLK] = terms[i, 0:KBLK]
        total[i, KBLK : 2 * KBLK] = jnp.zeros((KBLK, HD), jnp.float32)
    for j, d in enumerate(distances):

        @pl.when(me + d < ctx_count)
        def _(j=j, d=d):
            sel_copy(j, d).wait_recv()
            term_copy(j, d).wait_recv()
            where = jnp.broadcast_to(sel_in[j, 0:1], (KBLK, HD))
            for i in range(2):
                term = terms_in[j, i * KBLK : (i + 1) * KBLK].astype(jnp.float32)
                total[i, 0:KBLK] += jnp.where(where == 0, term, 0.0)
                total[i, KBLK : 2 * KBLK] += jnp.where(where == 1, term, 0.0)

    gk_store = pltpu.make_async_copy(total.at[0], gk_hbm, store_sem.at[1])
    gv_store = pltpu.make_async_copy(total.at[1], gv_hbm, store_sem.at[2])
    gk_store.start()
    gv_store.start()

    for j, d in enumerate(distances):

        @pl.when(me + d < ctx_count)
        def _(j=j, d=d):
            k_copy(j, d).wait_send()
            v_copy(j, d).wait_send()

        @pl.when(me - d >= 0)
        def _(j=j, d=d):
            sel_copy(j, d).wait_send()
            term_copy(j, d).wait_send()

    for c in range(chunks):
        for r in range(1, kvh_count):
            gq_copy(c, r).wait()
    gq_store.wait()
    att_store.wait()
    gk_store.wait()
    gv_store.wait()


def solution(mesh):
    ctx_count = mesh.shape["ctx"]
    kvh_count = mesh.shape["kvh"]
    distances = [1 << j for j in range(SLOTS - 1) if 1 << j < ctx_count]
    far = len(distances)
    slots = 1 + far

    def on_device(queries, keys, values, upstream, selected, counts):
        tokens, width = queries.shape
        key_rows = keys.shape[0]
        assert tokens == QBLK and key_rows == 2 * KBLK and selected.shape[0] == 1
        chunks = GROUP // PAIR
        bf16, f32 = jnp.bfloat16, jnp.float32
        dma = pltpu.SemaphoreType.DMA
        smem = pl.BlockSpec(memory_space=pltpu.SMEM)
        anywhere = pl.BlockSpec(memory_space=pl.ANY)
        return pl.pallas_call(
            functools.partial(kernel, ctx_count, kvh_count, distances),
            out_shape=(
                jax.ShapeDtypeStruct((tokens, width), bf16),
                jax.ShapeDtypeStruct((tokens // kvh_count, width * kvh_count), bf16),
                jax.ShapeDtypeStruct((key_rows, HD), f32),
                jax.ShapeDtypeStruct((key_rows, HD), f32),
            ),
            in_specs=[smem, smem] + [anywhere] * 4,
            out_specs=[anywhere] * 4,
            scratch_shapes=[
                pltpu.VMEM((tokens, width), bf16),
                pltpu.VMEM((tokens, width), bf16),
                pltpu.VMEM((key_rows, HD), bf16),
                pltpu.VMEM((key_rows, HD), bf16),
                pltpu.VMEM((far, key_rows, HD), bf16),
                pltpu.VMEM((far, key_rows, HD), bf16),
                pltpu.VMEM((far, 8, HD), jnp.int32),
                pltpu.VMEM((far, 8, HD), jnp.int32),
                pltpu.VMEM((slots * KBLK, HD), bf16),
                pltpu.VMEM((slots * KBLK, HD), bf16),
                pltpu.VMEM((tokens, width), bf16),
                pltpu.VMEM((tokens, width), bf16),
                pltpu.VMEM((2, slots * KBLK, HD), f32),
                pltpu.VMEM((far, 2 * KBLK, HD), bf16),
                pltpu.VMEM((far, 2 * KBLK, HD), bf16),
                pltpu.VMEM((2, key_rows, HD), f32),
                dma((4,)),
                dma((3,)),
                dma((2, far)),
                dma((2, far)),
                dma((far,)),
                dma((far,)),
                dma((far,)),
                dma((far,)),
                dma((chunks, kvh_count - 1)),
                dma((chunks, kvh_count - 1)),
                dma,
            ],
            compiler_params=pltpu.CompilerParams(
                collective_id=0, has_side_effects=True, vmem_limit_bytes=32 * 1024 * 1024
            ),
        )(selected, counts, queries, keys, values, upstream)

    placed = (
        P("ctx", "kvh"),
        P("ctx", "kvh"),
        P("ctx", "kvh"),
        P("ctx", "kvh"),
        P("ctx", None),
        P("ctx"),
    )
    return jax.shard_map(
        on_device,
        mesh=mesh,
        in_specs=placed,
        out_specs=(P("ctx", "kvh"), P(("ctx", "kvh"), None), P("ctx", "kvh"), P("ctx", "kvh")),
        check_vma=False,
    )
```

```python
import functools
import math

import jax
import jax.numpy as jnp
from jax import lax
from jax.experimental import pallas as pl
from jax.experimental.pallas import tpu as pltpu
from jax.sharding import PartitionSpec as P

HD = 128
GROUP = 8
KBLK = 64
QBLK = 128
SLOTS = 8
PAIR = 2

MESH = pl.DeviceIdType.MESH
LOG2E = math.log2(math.e)
NN = (((1,), (0,)), ((), ()))


def dot(a, b, dims):
    return lax.dot_general(a, b, dims, preferred_element_type=jnp.float32)


def kernel(
    ctx_count,
    kvh_count,
    distances,
    cnt_ref,
    sel_hbm,
    q_hbm,
    k_hbm,
    v_hbm,
    u_hbm,
    att_out,
    gq_out,
    own_out,
    terms_in,
    sel_in,
    sel_ref,
    q_v,
    u_v,
    q_t,
    u_t,
    k_own,
    v_own,
    k_in,
    v_in,
    sel_out,
    keys,
    vals,
    prob,
    prob_half,
    grad_scores,
    att_v,
    gq_v,
    own,
    terms_out,
    load_sem,
    store_sem,
    kv_send,
    kv_recv,
    sel_send,
    sel_recv,
    term_send,
    term_recv,
    gq_send,
    gq_recv,
):
    score_scale = 1.0 / math.sqrt(HD)
    bf16, f32 = jnp.bfloat16, jnp.float32
    me = lax.axis_index("ctx")
    head = lax.axis_index("kvh")
    slots = 1 + len(distances)
    part = QBLK // kvh_count
    width = GROUP * HD
    chunks = GROUP // PAIR
    lanes = PAIR * QBLK

    loads = [
        pltpu.make_async_copy(src, dst, load_sem.at[i])
        for i, (src, dst) in enumerate(
            [
                (sel_hbm, sel_ref),
                (k_hbm, k_own),
                (v_hbm, v_own),
                (q_hbm, q_v),
                (u_hbm, u_v),
            ]
        )
    ]
    for copy in loads:
        copy.start()

    barrier = pltpu.get_barrier_semaphore()
    for r in range(1, kvh_count):
        peer = lax.rem(head + r, kvh_count)
        pl.semaphore_signal(barrier, inc=1, device_id={"kvh": peer}, device_id_type=MESH)
    for d in distances:

        @pl.when(me + d < ctx_count)
        def _():
            pl.semaphore_signal(barrier, inc=1, device_id={"ctx": me + d}, device_id_type=MESH)

        @pl.when(me - d >= 0)
        def _():
            pl.semaphore_signal(barrier, inc=1, device_id={"ctx": me - d}, device_id_type=MESH)

    for copy in loads[:3]:
        copy.wait()
    for j, d in enumerate(distances):
        sel_out[j] = jnp.full((8, HD), sel_ref[0, j + 1] - 2 * (me - d), jnp.int32)

    partners = kvh_count - 1
    for d in distances:
        partners += 1 - (me + d) // ctx_count + (me - d + ctx_count) // ctx_count
    pl.semaphore_wait(barrier, partners)

    def remote(src, dst, send, recv, **where):
        return pltpu.make_async_remote_copy(
            src_ref=src, dst_ref=dst, send_sem=send, recv_sem=recv,
            device_id=where, device_id_type=MESH,
        )

    def k_copy(j, d):
        return remote(k_own, k_in.at[j], kv_send.at[0, j], kv_recv.at[0, j], ctx=me + d)

    def v_copy(j, d):
        return remote(v_own, v_in.at[j], kv_send.at[1, j], kv_recv.at[1, j], ctx=me + d)

    def sel_copy(j, d):
        return remote(sel_out.at[j], sel_in.at[j], sel_send.at[j], sel_recv.at[j], ctx=me - d)

    def term_copy(i, j, d):
        return remote(
            terms_out.at[i, j], terms_in.at[i, j], term_send.at[i, j], term_recv.at[i, j], ctx=me - d
        )

    def gq_copy(c, r):
        cols = PAIR * HD
        peer = lax.rem(head + r, kvh_count)
        return remote(
            gq_v.at[pl.ds(pl.multiple_of(peer * part, part), part), pl.ds(c * cols, cols)],
            gq_out.at[:, pl.ds(pl.multiple_of(head * width + c * cols, cols), cols)],
            gq_send.at[c, r - 1],
            gq_recv.at[c, r - 1],
            kvh=peer,
        )

    by_far = list(enumerate(distances))[::-1]
    for make in (k_copy, v_copy):
        for j, d in by_far:

            @pl.when(me + d < ctx_count)
            def _(make=make, j=j, d=d):
                make(j, d).start()

    for j, d in by_far:

        @pl.when(me - d >= 0)
        def _(j=j, d=d):
            sel_copy(j, d).start()

    for copy in loads[3:]:
        copy.wait()
    for h in range(GROUP):
        at = slice(h * HD, (h + 1) * HD)
        q_t[:, at] = q_v[:, at].astype(f32).T.astype(bf16)
        u_t[:, at] = u_v[:, at].astype(f32).T.astype(bf16)

    count = cnt_ref[0]

    def receive(make, own_rows, arrived, chosen):
        chosen[0:KBLK] = own_rows[0:KBLK]
        for j, d in enumerate(distances):

            @pl.when(me - d >= 0)
            def _(j=j, d=d):
                make(j, d).wait_recv()

            live = jnp.full((KBLK, HD), count > j + 1)
            upper = jnp.full((KBLK, HD), sel_ref[0, j + 1] - 2 * (me - d) > 0)
            lo = arrived[j, 0:KBLK].astype(f32)
            hi = arrived[j, KBLK : 2 * KBLK].astype(f32)
            rows = jnp.where(live, jnp.where(upper, hi, lo), 0.0)
            chosen[(j + 1) * KBLK : (j + 2) * KBLK] = rows.astype(bf16)
        return chosen[...]

    def send_terms(i, term):
        own[i] = term[0:KBLK]
        for j, d in by_far:
            terms_out[i, j] = term[(j + 1) * KBLK : (j + 2) * KBLK].astype(bf16)

            @pl.when(me - d >= 0)
            def _(j=j, d=d):
                term_copy(i, j, d).start()

    def by_rows(ref):
        return jnp.concatenate([ref[:, h * HD : (h + 1) * HD] for h in range(GROUP)], axis=0)

    k_all = receive(k_copy, k_own, k_in, keys)
    key_at = lax.broadcasted_iota(jnp.int32, (KBLK, lanes), 0)
    query_at = lax.rem(lax.broadcasted_iota(jnp.int32, (KBLK, lanes), 1), QBLK)
    causal = key_at <= query_at
    hidden = [jnp.full((KBLK, lanes), count <= j) for j in range(1, slots)]
    for c in range(chunks):
        at = slice(c * lanes, (c + 1) * lanes)
        s = dot(k_all, q_t[:, at], NN)
        s = jnp.concatenate(
            [jnp.where(causal, s[0:KBLK], -1e30)]
            + [
                jnp.where(hidden[j - 1], -1e30, s[j * KBLK : (j + 1) * KBLK])
                for j in range(1, slots)
            ],
            axis=0,
        )
        peak = jnp.max(s, axis=0, keepdims=True)
        e = jnp.exp2((s - peak) * (score_scale * LOG2E))
        p = e * (1.0 / jnp.sum(e, axis=0, keepdims=True))
        prob[:, at] = p
        prob_half[:, at] = p.astype(bf16)
    send_terms(1, dot(prob_half[...], by_rows(u_v), NN))

    v_all = receive(v_copy, v_own, v_in, vals)
    k_t = k_all.astype(f32).T.astype(bf16)
    for c in range(chunks):
        at = slice(c * lanes, (c + 1) * lanes)
        dp = dot(v_all, u_t[:, at], NN)
        p = prob[:, at]
        row_term = jnp.sum(p * dp, axis=0, keepdims=True)
        ds = (p * (dp - row_term)).astype(bf16)
        grad_scores[:, at] = ds
        gq_c = dot(k_t, ds, NN) * score_scale
        for i in range(PAIR):
            h = c * PAIR + i
            gq_v[:, h * HD : (h + 1) * HD] = gq_c[:, i * QBLK : (i + 1) * QBLK].T.astype(bf16)
        for r in range(1, kvh_count):
            gq_copy(c, r).start()
    send_terms(0, dot(grad_scores[...], by_rows(q_v), NN) * score_scale)

    v_t = v_all.astype(f32).T.astype(bf16)
    for c in range(chunks):
        at = slice(c * lanes, (c + 1) * lanes)
        att_c = dot(v_t, prob_half[:, at], NN)
        for i in range(PAIR):
            h = c * PAIR + i
            att_v[:, h * HD : (h + 1) * HD] = att_c[:, i * QBLK : (i + 1) * QBLK].T.astype(bf16)

    stores = [
        pltpu.make_async_copy(
            gq_v.at[pl.ds(pl.multiple_of(head * part, part), part), :],
            gq_out.at[:, pl.ds(pl.multiple_of(head * width, width), width)],
            store_sem.at[0],
        ),
        pltpu.make_async_copy(own, own_out, store_sem.at[1]),
        pltpu.make_async_copy(att_v, att_out, store_sem.at[2]),
    ]
    for copy in stores:
        copy.start()

    for j, d in enumerate(distances):

        @pl.when(me + d < ctx_count)
        def _(j=j, d=d):
            k_copy(j, d).wait_send()
            v_copy(j, d).wait_send()
            sel_copy(j, d).wait_recv()
            term_copy(1, j, d).wait_recv()
            term_copy(0, j, d).wait_recv()

        @pl.when(me - d >= 0)
        def _(j=j, d=d):
            sel_copy(j, d).wait_send()
            term_copy(1, j, d).wait_send()
            term_copy(0, j, d).wait_send()

    for c in range(chunks):
        for r in range(1, kvh_count):
            gq_copy(c, r).wait()
    for copy in stores:
        copy.wait()


def finish(ctx_count, distances, att, gq, own, terms, sel, att_hbm, gq_hbm, gk_hbm, gv_hbm, total, sem):
    me = lax.axis_index("ctx")
    stores = [
        pltpu.make_async_copy(src, dst, sem.at[i])
        for i, (src, dst) in enumerate(
            [(att, att_hbm), (gq, gq_hbm), (total.at[0], gk_hbm), (total.at[1], gv_hbm)]
        )
    ]
    stores[0].start()
    stores[1].start()
    for i in range(2):
        total[i, 0:KBLK] = own[i]
        total[i, KBLK : 2 * KBLK] = jnp.zeros((KBLK, HD), jnp.float32)
    for j, d in enumerate(distances):

        @pl.when(me + d < ctx_count)
        def _(j=j, d=d):
            where = jnp.broadcast_to(sel[j, 0:1], (KBLK, HD))
            for i in range(2):
                term = terms[i, j].astype(jnp.float32)
                total[i, 0:KBLK] += jnp.where(where == 0, term, 0.0)
                total[i, KBLK : 2 * KBLK] += jnp.where(where == 1, term, 0.0)

    stores[2].start()
    stores[3].start()
    for copy in stores:
        copy.wait()


def solution(mesh):
    ctx_count = mesh.shape["ctx"]
    kvh_count = mesh.shape["kvh"]
    distances = [1 << j for j in range(SLOTS - 1) if 1 << j < ctx_count]
    far = len(distances)
    slots = 1 + far

    def on_device(queries, keys, values, upstream, selected, counts):
        tokens, width = queries.shape
        key_rows = keys.shape[0]
        assert tokens == QBLK and key_rows == 2 * KBLK and selected.shape[0] == 1
        chunks = GROUP // PAIR
        bf16, f32 = jnp.bfloat16, jnp.float32
        dma = pltpu.SemaphoreType.DMA
        smem = pl.BlockSpec(memory_space=pltpu.SMEM)
        hbm = pl.BlockSpec(memory_space=pltpu.HBM)
        vmem = pl.BlockSpec(memory_space=pltpu.VMEM)
        anywhere = pl.BlockSpec(memory_space=pl.ANY)
        result = [
            jax.ShapeDtypeStruct((tokens, width), bf16),
            jax.ShapeDtypeStruct((tokens // kvh_count, width * kvh_count), bf16),
        ]
        grad = jax.ShapeDtypeStruct((key_rows, HD), f32)
        parts = pl.pallas_call(
            functools.partial(kernel, ctx_count, kvh_count, distances),
            out_shape=result
            + [
                jax.ShapeDtypeStruct((2, KBLK, HD), f32),
                jax.ShapeDtypeStruct((2, far, KBLK, HD), bf16),
                jax.ShapeDtypeStruct((far, 8, HD), jnp.int32),
            ],
            in_specs=[smem] + [hbm] * 5,
            out_specs=[anywhere] * 5,
            scratch_shapes=[
                pltpu.SMEM((1, SLOTS), jnp.int32),
                pltpu.VMEM((tokens, width), bf16),
                pltpu.VMEM((tokens, width), bf16),
                pltpu.VMEM((HD, GROUP * tokens), bf16),
                pltpu.VMEM((HD, GROUP * tokens), bf16),
                pltpu.VMEM((key_rows, HD), bf16),
                pltpu.VMEM((key_rows, HD), bf16),
                pltpu.VMEM((far, key_rows, HD), bf16),
                pltpu.VMEM((far, key_rows, HD), bf16),
                pltpu.VMEM((far, 8, HD), jnp.int32),
                pltpu.VMEM((slots * KBLK, HD), bf16),
                pltpu.VMEM((slots * KBLK, HD), bf16),
                pltpu.VMEM((slots * KBLK, GROUP * tokens), f32),
                pltpu.VMEM((slots * KBLK, GROUP * tokens), bf16),
                pltpu.VMEM((slots * KBLK, GROUP * tokens), bf16),
                pltpu.VMEM((tokens, width), bf16),
                pltpu.VMEM((tokens, width), bf16),
                pltpu.VMEM((2, KBLK, HD), f32),
                pltpu.VMEM((2, far, KBLK, HD), bf16),
                dma((5,)),
                dma((3,)),
                dma((2, far)),
                dma((2, far)),
                dma((far,)),
                dma((far,)),
                dma((2, far)),
                dma((2, far)),
                dma((chunks, kvh_count - 1)),
                dma((chunks, kvh_count - 1)),
            ],
            compiler_params=pltpu.CompilerParams(
                collective_id=0, has_side_effects=True, vmem_limit_bytes=32 * 1024 * 1024
            ),
        )(
            counts,
            *[
                pltpu.with_memory_space_constraint(x, pltpu.HBM)
                for x in (selected, queries, keys, values, upstream)
            ],
        )
        return pl.pallas_call(
            functools.partial(finish, ctx_count, distances),
            out_shape=result + [grad, grad],
            in_specs=[anywhere, anywhere, vmem, vmem, vmem],
            out_specs=[hbm] * 4,
            scratch_shapes=[pltpu.VMEM((2, key_rows, HD), f32), dma((4,))],
        )(*parts)

    placed = (
        P("ctx", "kvh"),
        P("ctx", "kvh"),
        P("ctx", "kvh"),
        P("ctx", "kvh"),
        P("ctx", None),
        P("ctx"),
    )
    return jax.shard_map(
        on_device,
        mesh=mesh,
        in_specs=placed,
        out_specs=(P("ctx", "kvh"), P(("ctx", "kvh"), None), P("ctx", "kvh"), P("ctx", "kvh")),
        check_vma=False,
    )
```

```python
import functools
import math

import jax
import jax.numpy as jnp
from jax import lax
from jax.experimental import pallas as pl
from jax.experimental.pallas import tpu as pltpu
from jax.sharding import PartitionSpec as P

HD = 128
GROUP = 8
KBLK = 64
QBLK = 128
SLOTS = 8
PAIR = 2

MESH = pl.DeviceIdType.MESH
LOG2E = math.log2(math.e)
NN = (((1,), (0,)), ((), ()))


def dot(a, b, dims):
    return lax.dot_general(a, b, dims, preferred_element_type=jnp.float32)


def kernel(
    ctx_count,
    kvh_count,
    distances,
    cnt_ref,
    sel_hbm,
    q_hbm,
    k_hbm,
    v_hbm,
    u_hbm,
    att_out,
    gq_out,
    own_out,
    terms_in,
    sel_store,
    sel_ref,
    q_v,
    u_v,
    q_t,
    u_t,
    k_own,
    v_own,
    k_out,
    v_out,
    k_in,
    v_in,
    sel_out,
    sel_in,
    keys,
    vals,
    prob,
    prob_half,
    grad_scores,
    att_v,
    gq_v,
    own,
    terms_out,
    load_sem,
    store_sem,
    kv_send,
    kv_recv,
    sel_send,
    sel_recv,
    term_send,
    term_recv,
    gq_send,
    gq_recv,
):
    score_scale = 1.0 / math.sqrt(HD)
    bf16, f32 = jnp.bfloat16, jnp.float32
    me = lax.axis_index("ctx")
    head = lax.axis_index("kvh")
    slots = 1 + len(distances)
    part = QBLK // kvh_count
    width = GROUP * HD
    chunks = GROUP // PAIR
    lanes = PAIR * QBLK

    loads = [
        pltpu.make_async_copy(src, dst, load_sem.at[i])
        for i, (src, dst) in enumerate(
            [
                (sel_hbm, sel_ref),
                (k_hbm, k_own),
                (v_hbm, v_own),
                (q_hbm, q_v),
                (u_hbm, u_v),
            ]
        )
    ]
    for copy in loads:
        copy.start()

    barrier = pltpu.get_barrier_semaphore()
    for r in range(1, kvh_count):
        peer = lax.rem(head + r, kvh_count)
        pl.semaphore_signal(barrier, inc=1, device_id={"kvh": peer}, device_id_type=MESH)
    for d in distances:

        @pl.when(me + d < ctx_count)
        def _():
            pl.semaphore_signal(barrier, inc=1, device_id={"ctx": me + d}, device_id_type=MESH)

        @pl.when(me - d >= 0)
        def _():
            pl.semaphore_signal(barrier, inc=1, device_id={"ctx": me - d}, device_id_type=MESH)

    for copy in loads[:3]:
        copy.wait()
    for j, d in enumerate(distances):
        sel_out[j] = jnp.full((8, HD), sel_ref[0, j + 1] - 2 * (me - d), jnp.int32)

    partners = kvh_count - 1
    for d in distances:
        partners += 1 - (me + d) // ctx_count + (me - d + ctx_count) // ctx_count
    pl.semaphore_wait(barrier, partners)

    def remote(src, dst, send, recv, **where):
        return pltpu.make_async_remote_copy(
            src_ref=src, dst_ref=dst, send_sem=send, recv_sem=recv,
            device_id=where, device_id_type=MESH,
        )

    def k_copy(j, d):
        return remote(k_out.at[j], k_in.at[j], kv_send.at[0, j], kv_recv.at[0, j], ctx=me + d)

    def v_copy(j, d):
        return remote(v_out.at[j], v_in.at[j], kv_send.at[1, j], kv_recv.at[1, j], ctx=me + d)

    def sel_copy(j, d):
        return remote(sel_out.at[j], sel_in.at[j], sel_send.at[j], sel_recv.at[j], ctx=me - d)

    def term_copy(i, j, d):
        return remote(
            terms_out.at[i, j], terms_in.at[i, j], term_send.at[i, j], term_recv.at[i, j], ctx=me - d
        )

    def gq_copy(c, r):
        cols = PAIR * HD
        peer = lax.rem(head + r, kvh_count)
        return remote(
            gq_v.at[pl.ds(pl.multiple_of(peer * part, part), part), pl.ds(c * cols, cols)],
            gq_out.at[:, pl.ds(pl.multiple_of(head * width + c * cols, cols), cols)],
            gq_send.at[c, r - 1],
            gq_recv.at[c, r - 1],
            kvh=peer,
        )

    by_far = list(enumerate(distances))[::-1]
    for j, d in by_far:

        @pl.when(me - d >= 0)
        def _(j=j, d=d):
            sel_copy(j, d).start()

    for copy in loads[3:]:
        copy.wait()

    def transpose(rows, columns):
        for h in range(GROUP):
            at = slice(h * HD, (h + 1) * HD)
            columns[:, at] = rows[:, at].astype(f32).T.astype(bf16)

    def send_rows(make, own_rows, out, first):
        for j, d in enumerate(distances):

            @pl.when(me + d < ctx_count)
            def _(j=j, d=d):
                if first:
                    sel_copy(j, d).wait_recv()
                upper = jnp.broadcast_to(sel_in[j, 0:1], (KBLK, HD)) > 0
                lo = own_rows[0:KBLK].astype(f32)
                hi = own_rows[KBLK : 2 * KBLK].astype(f32)
                out[j] = jnp.where(upper, hi, lo).astype(bf16)
                make(j, d).start()

    transpose(q_v, q_t)
    send_rows(k_copy, k_own, k_out, True)
    send_rows(v_copy, v_own, v_out, False)
    transpose(u_v, u_t)

    count = cnt_ref[0]

    def receive(make, own_rows, arrived, chosen):
        chosen[0:KBLK] = own_rows[0:KBLK]
        for j, d in enumerate(distances):

            @pl.when(me - d >= 0)
            def _(j=j, d=d):
                make(j, d).wait_recv()

            live = jnp.full((KBLK, HD), count > j + 1)
            rows = jnp.where(live, arrived[j].astype(f32), 0.0)
            chosen[(j + 1) * KBLK : (j + 2) * KBLK] = rows.astype(bf16)
        return chosen[...]

    def send_terms(i, term):
        own[i] = term[0:KBLK]
        for j, d in by_far:
            terms_out[i, j] = term[(j + 1) * KBLK : (j + 2) * KBLK].astype(bf16)

            @pl.when(me - d >= 0)
            def _(j=j, d=d):
                term_copy(i, j, d).start()

    def by_rows(ref):
        return jnp.concatenate([ref[:, h * HD : (h + 1) * HD] for h in range(GROUP)], axis=0)

    k_all = receive(k_copy, k_own, k_in, keys)
    key_at = lax.broadcasted_iota(jnp.int32, (KBLK, lanes), 0)
    query_at = lax.rem(lax.broadcasted_iota(jnp.int32, (KBLK, lanes), 1), QBLK)
    causal = key_at <= query_at
    hidden = [jnp.full((KBLK, lanes), count <= j) for j in range(1, slots)]
    for c in range(chunks):
        at = slice(c * lanes, (c + 1) * lanes)
        s = dot(k_all, q_t[:, at], NN)
        s = jnp.concatenate(
            [jnp.where(causal, s[0:KBLK], -1e30)]
            + [
                jnp.where(hidden[j - 1], -1e30, s[j * KBLK : (j + 1) * KBLK])
                for j in range(1, slots)
            ],
            axis=0,
        )
        peak = jnp.max(s, axis=0, keepdims=True)
        e = jnp.exp2((s - peak) * (score_scale * LOG2E))
        p = e * (1.0 / jnp.sum(e, axis=0, keepdims=True))
        prob[:, at] = p
        prob_half[:, at] = p.astype(bf16)
    send_terms(1, dot(prob_half[...], by_rows(u_v), NN))

    v_all = receive(v_copy, v_own, v_in, vals)
    k_t = k_all.astype(f32).T.astype(bf16)
    for c in range(chunks):
        at = slice(c * lanes, (c + 1) * lanes)
        dp = dot(v_all, u_t[:, at], NN)
        p = prob[:, at]
        row_term = jnp.sum(p * dp, axis=0, keepdims=True)
        ds = (p * (dp - row_term)).astype(bf16)
        grad_scores[:, at] = ds
        gq_c = dot(k_t, ds, NN) * score_scale
        for i in range(PAIR):
            h = c * PAIR + i
            gq_v[:, h * HD : (h + 1) * HD] = gq_c[:, i * QBLK : (i + 1) * QBLK].T.astype(bf16)
        for r in range(1, kvh_count):
            gq_copy(c, r).start()
    send_terms(0, dot(grad_scores[...], by_rows(q_v), NN) * score_scale)

    v_t = v_all.astype(f32).T.astype(bf16)
    for c in range(chunks):
        at = slice(c * lanes, (c + 1) * lanes)
        att_c = dot(v_t, prob_half[:, at], NN)
        for i in range(PAIR):
            h = c * PAIR + i
            att_v[:, h * HD : (h + 1) * HD] = att_c[:, i * QBLK : (i + 1) * QBLK].T.astype(bf16)

    stores = [
        pltpu.make_async_copy(
            gq_v.at[pl.ds(pl.multiple_of(head * part, part), part), :],
            gq_out.at[:, pl.ds(pl.multiple_of(head * width, width), width)],
            store_sem.at[0],
        ),
        pltpu.make_async_copy(own, own_out, store_sem.at[1]),
        pltpu.make_async_copy(att_v, att_out, store_sem.at[2]),
        pltpu.make_async_copy(sel_in, sel_store, store_sem.at[3]),
    ]
    for copy in stores:
        copy.start()

    for j, d in enumerate(distances):

        @pl.when(me + d < ctx_count)
        def _(j=j, d=d):
            k_copy(j, d).wait_send()
            v_copy(j, d).wait_send()
            term_copy(1, j, d).wait_recv()
            term_copy(0, j, d).wait_recv()

        @pl.when(me - d >= 0)
        def _(j=j, d=d):
            sel_copy(j, d).wait_send()
            term_copy(1, j, d).wait_send()
            term_copy(0, j, d).wait_send()

    for c in range(chunks):
        for r in range(1, kvh_count):
            gq_copy(c, r).wait()
    for copy in stores:
        copy.wait()


def finish(ctx_count, distances, att, gq, own, terms, sel, att_hbm, gq_hbm, gk_hbm, gv_hbm, total, sem):
    me = lax.axis_index("ctx")
    stores = [
        pltpu.make_async_copy(src, dst, sem.at[i])
        for i, (src, dst) in enumerate(
            [(att, att_hbm), (gq, gq_hbm), (total.at[0], gk_hbm), (total.at[1], gv_hbm)]
        )
    ]
    stores[0].start()
    stores[1].start()
    for i in range(2):
        total[i, 0:KBLK] = own[i]
        total[i, KBLK : 2 * KBLK] = jnp.zeros((KBLK, HD), jnp.float32)
    for j, d in enumerate(distances):

        @pl.when(me + d < ctx_count)
        def _(j=j, d=d):
            where = jnp.broadcast_to(sel[j, 0:1], (KBLK, HD))
            for i in range(2):
                term = terms[i, j].astype(jnp.float32)
                total[i, 0:KBLK] += jnp.where(where == 0, term, 0.0)
                total[i, KBLK : 2 * KBLK] += jnp.where(where == 1, term, 0.0)

    stores[2].start()
    stores[3].start()
    for copy in stores:
        copy.wait()


def solution(mesh):
    ctx_count = mesh.shape["ctx"]
    kvh_count = mesh.shape["kvh"]
    distances = [1 << j for j in range(SLOTS - 1) if 1 << j < ctx_count]
    far = len(distances)
    slots = 1 + far

    def on_device(queries, keys, values, upstream, selected, counts):
        tokens, width = queries.shape
        key_rows = keys.shape[0]
        assert tokens == QBLK and key_rows == 2 * KBLK and selected.shape[0] == 1
        chunks = GROUP // PAIR
        bf16, f32 = jnp.bfloat16, jnp.float32
        dma = pltpu.SemaphoreType.DMA
        smem = pl.BlockSpec(memory_space=pltpu.SMEM)
        hbm = pl.BlockSpec(memory_space=pltpu.HBM)
        vmem = pl.BlockSpec(memory_space=pltpu.VMEM)
        anywhere = pl.BlockSpec(memory_space=pl.ANY)
        result = [
            jax.ShapeDtypeStruct((tokens, width), bf16),
            jax.ShapeDtypeStruct((tokens // kvh_count, width * kvh_count), bf16),
        ]
        grad = jax.ShapeDtypeStruct((key_rows, HD), f32)
        parts = pl.pallas_call(
            functools.partial(kernel, ctx_count, kvh_count, distances),
            out_shape=result
            + [
                jax.ShapeDtypeStruct((2, KBLK, HD), f32),
                jax.ShapeDtypeStruct((2, far, KBLK, HD), bf16),
                jax.ShapeDtypeStruct((far, 8, HD), jnp.int32),
            ],
            in_specs=[smem] + [hbm] * 5,
            out_specs=[anywhere] * 5,
            scratch_shapes=[
                pltpu.SMEM((1, SLOTS), jnp.int32),
                pltpu.VMEM((tokens, width), bf16),
                pltpu.VMEM((tokens, width), bf16),
                pltpu.VMEM((HD, GROUP * tokens), bf16),
                pltpu.VMEM((HD, GROUP * tokens), bf16),
                pltpu.VMEM((key_rows, HD), bf16),
                pltpu.VMEM((key_rows, HD), bf16),
                pltpu.VMEM((far, KBLK, HD), bf16),
                pltpu.VMEM((far, KBLK, HD), bf16),
                pltpu.VMEM((far, KBLK, HD), bf16),
                pltpu.VMEM((far, KBLK, HD), bf16),
                pltpu.VMEM((far, 8, HD), jnp.int32),
                pltpu.VMEM((far, 8, HD), jnp.int32),
                pltpu.VMEM((slots * KBLK, HD), bf16),
                pltpu.VMEM((slots * KBLK, HD), bf16),
                pltpu.VMEM((slots * KBLK, GROUP * tokens), f32),
                pltpu.VMEM((slots * KBLK, GROUP * tokens), bf16),
                pltpu.VMEM((slots * KBLK, GROUP * tokens), bf16),
                pltpu.VMEM((tokens, width), bf16),
                pltpu.VMEM((tokens, width), bf16),
                pltpu.VMEM((2, KBLK, HD), f32),
                pltpu.VMEM((2, far, KBLK, HD), bf16),
                dma((5,)),
                dma((4,)),
                dma((2, far)),
                dma((2, far)),
                dma((far,)),
                dma((far,)),
                dma((2, far)),
                dma((2, far)),
                dma((chunks, kvh_count - 1)),
                dma((chunks, kvh_count - 1)),
            ],
            compiler_params=pltpu.CompilerParams(
                collective_id=0, has_side_effects=True, vmem_limit_bytes=32 * 1024 * 1024
            ),
        )(
            counts,
            *[
                pltpu.with_memory_space_constraint(x, pltpu.HBM)
                for x in (selected, queries, keys, values, upstream)
            ],
        )
        return pl.pallas_call(
            functools.partial(finish, ctx_count, distances),
            out_shape=result + [grad, grad],
            in_specs=[anywhere, anywhere, vmem, vmem, vmem],
            out_specs=[hbm] * 4,
            scratch_shapes=[pltpu.VMEM((2, key_rows, HD), f32), dma((4,))],
            compiler_params=pltpu.CompilerParams(vmem_limit_bytes=4 * 1024 * 1024),
        )(*parts)

    placed = (
        P("ctx", "kvh"),
        P("ctx", "kvh"),
        P("ctx", "kvh"),
        P("ctx", "kvh"),
        P("ctx", None),
        P("ctx"),
    )
    return jax.shard_map(
        on_device,
        mesh=mesh,
        in_specs=placed,
        out_specs=(P("ctx", "kvh"), P(("ctx", "kvh"), None), P("ctx", "kvh"), P("ctx", "kvh")),
        check_vma=False,
    )
```

```python
import functools
import math

import jax
import jax.numpy as jnp
from jax import lax
from jax.experimental import pallas as pl
from jax.experimental.pallas import tpu as pltpu
from jax.sharding import PartitionSpec as P

HD = 128
GROUP = 8
KBLK = 64
QBLK = 128
SLOTS = 8
PAIR = 2

MESH = pl.DeviceIdType.MESH
LOG2E = math.log2(math.e)
NN = (((1,), (0,)), ((), ()))


def dot(a, b, dims):
    return lax.dot_general(a, b, dims, preferred_element_type=jnp.float32)


def kernel(
    ctx_count,
    kvh_count,
    distances,
    cnt_ref,
    sel_hbm,
    q_hbm,
    k_hbm,
    v_hbm,
    u_hbm,
    att_out,
    gq_out,
    own_out,
    terms_in,
    sel_store,
    sel_ref,
    q_v,
    u_v,
    q_t,
    u_t,
    k_own,
    v_own,
    k_out,
    v_out,
    k_in,
    v_in,
    sel_out,
    sel_in,
    keys,
    vals,
    prob,
    prob_half,
    grad_scores,
    att_v,
    gq_v,
    own,
    terms_out,
    load_sem,
    store_sem,
    kv_send,
    kv_recv,
    sel_send,
    sel_recv,
    term_send,
    term_recv,
    gq_send,
    gq_recv,
):
    score_scale = 1.0 / math.sqrt(HD)
    bf16, f32 = jnp.bfloat16, jnp.float32
    me = lax.axis_index("ctx")
    head = lax.axis_index("kvh")
    slots = 1 + len(distances)
    part = QBLK // kvh_count
    width = GROUP * HD
    chunks = GROUP // PAIR
    lanes = PAIR * QBLK

    loads = [
        pltpu.make_async_copy(src, dst, load_sem.at[i])
        for i, (src, dst) in enumerate(
            [
                (sel_hbm, sel_ref),
                (k_hbm, k_own),
                (v_hbm, v_own),
                (q_hbm, q_v),
                (u_hbm, u_v),
            ]
        )
    ]
    for copy in loads:
        copy.start()

    barrier = pltpu.get_barrier_semaphore()
    for r in range(1, kvh_count):
        peer = lax.rem(head + r, kvh_count)
        pl.semaphore_signal(barrier, inc=1, device_id={"kvh": peer}, device_id_type=MESH)
    for d in distances:

        @pl.when(me + d < ctx_count)
        def _():
            pl.semaphore_signal(barrier, inc=1, device_id={"ctx": me + d}, device_id_type=MESH)

        @pl.when(me - d >= 0)
        def _():
            pl.semaphore_signal(barrier, inc=1, device_id={"ctx": me - d}, device_id_type=MESH)

    for copy in loads[:3]:
        copy.wait()
    for j, d in enumerate(distances):
        sel_out[j] = jnp.full((8, HD), sel_ref[0, j + 1] - 2 * (me - d), jnp.int32)

    partners = kvh_count - 1
    for d in distances:
        partners += 1 - (me + d) // ctx_count + (me - d + ctx_count) // ctx_count
    pl.semaphore_wait(barrier, partners)

    def remote(src, dst, send, recv, **where):
        return pltpu.make_async_remote_copy(
            src_ref=src, dst_ref=dst, send_sem=send, recv_sem=recv,
            device_id=where, device_id_type=MESH,
        )

    def k_copy(j, d):
        return remote(k_out.at[j], k_in.at[j], kv_send.at[0, j], kv_recv.at[0, j], ctx=me + d)

    def v_copy(j, d):
        return remote(v_out.at[j], v_in.at[j], kv_send.at[1, j], kv_recv.at[1, j], ctx=me + d)

    def sel_copy(j, d):
        return remote(sel_out.at[j], sel_in.at[j], sel_send.at[j], sel_recv.at[j], ctx=me - d)

    def term_copy(i, j, d):
        return remote(
            terms_out.at[i, j], terms_in.at[i, j], term_send.at[i, j], term_recv.at[i, j], ctx=me - d
        )

    def gq_copy(c, r):
        cols = PAIR * HD
        peer = lax.rem(head + r, kvh_count)
        return remote(
            gq_v.at[pl.ds(pl.multiple_of(peer * part, part), part), pl.ds(c * cols, cols)],
            gq_out.at[:, pl.ds(pl.multiple_of(head * width + c * cols, cols), cols)],
            gq_send.at[c, r - 1],
            gq_recv.at[c, r - 1],
            kvh=peer,
        )

    by_far = list(enumerate(distances))[::-1]
    for j, d in by_far:

        @pl.when(me - d >= 0)
        def _(j=j, d=d):
            sel_copy(j, d).start()

    for copy in loads[3:]:
        copy.wait()

    def transpose(rows, columns):
        for h in range(GROUP):
            at = slice(h * HD, (h + 1) * HD)
            columns[:, at] = rows[:, at].astype(f32).T.astype(bf16)

    def send_rows(make, own_rows, out, first):
        for j, d in enumerate(distances):

            @pl.when(me + d < ctx_count)
            def _(j=j, d=d):
                if first:
                    sel_copy(j, d).wait_recv()
                upper = jnp.broadcast_to(sel_in[j, 0:1], (KBLK, HD)) > 0
                lo = own_rows[0:KBLK].astype(f32)
                hi = own_rows[KBLK : 2 * KBLK].astype(f32)
                out[j] = jnp.where(upper, hi, lo).astype(bf16)
                make(j, d).start()

    transpose(q_v, q_t)
    send_rows(k_copy, k_own, k_out, True)
    send_rows(v_copy, v_own, v_out, False)
    transpose(u_v, u_t)

    count = cnt_ref[0]

    def receive(make, own_rows, arrived, chosen):
        chosen[0:KBLK] = own_rows[0:KBLK]
        for j, d in enumerate(distances):

            @pl.when(me - d >= 0)
            def _(j=j, d=d):
                make(j, d).wait_recv()

            live = jnp.full((KBLK, HD), count > j + 1)
            rows = jnp.where(live, arrived[j].astype(f32), 0.0)
            chosen[(j + 1) * KBLK : (j + 2) * KBLK] = rows.astype(bf16)
        return chosen[...]

    def send_terms(i, term):
        own[i] = term[0:KBLK]
        for j, d in by_far:
            terms_out[i, j] = term[(j + 1) * KBLK : (j + 2) * KBLK].astype(bf16)

            @pl.when(me - d >= 0)
            def _(j=j, d=d):
                term_copy(i, j, d).start()

    def by_rows(ref):
        return jnp.concatenate([ref[:, h * HD : (h + 1) * HD] for h in range(GROUP)], axis=0)

    k_all = receive(k_copy, k_own, k_in, keys)
    key_at = lax.broadcasted_iota(jnp.int32, (KBLK, lanes), 0)
    query_at = lax.rem(lax.broadcasted_iota(jnp.int32, (KBLK, lanes), 1), QBLK)
    causal = key_at <= query_at
    hidden = [jnp.full((KBLK, lanes), count <= j) for j in range(1, slots)]
    for c in range(chunks):
        at = slice(c * lanes, (c + 1) * lanes)
        s = dot(k_all, q_t[:, at], NN)
        s = jnp.concatenate(
            [jnp.where(causal, s[0:KBLK], -1e30)]
            + [
                jnp.where(hidden[j - 1], -1e30, s[j * KBLK : (j + 1) * KBLK])
                for j in range(1, slots)
            ],
            axis=0,
        )
        peak = jnp.max(s, axis=0, keepdims=True)
        e = jnp.exp2((s - peak) * (score_scale * LOG2E))
        p = e * (1.0 / jnp.sum(e, axis=0, keepdims=True))
        prob[:, at] = p
        prob_half[:, at] = p.astype(bf16)
    send_terms(1, dot(prob_half[...], by_rows(u_v), NN))

    v_all = receive(v_copy, v_own, v_in, vals)
    for c in range(chunks):
        at = slice(c * lanes, (c + 1) * lanes)
        dp = dot(v_all, u_t[:, at], NN)
        p = prob[:, at]
        row_term = jnp.sum(p * dp, axis=0, keepdims=True)
        ds = (p * (dp - row_term)).astype(bf16)
        grad_scores[:, at] = ds
    send_terms(0, dot(grad_scores[...], by_rows(q_v), NN) * score_scale)

    k_t = k_all.astype(f32).T.astype(bf16)
    for c in range(chunks):
        at = slice(c * lanes, (c + 1) * lanes)
        gq_c = dot(k_t, grad_scores[:, at], NN) * score_scale
        for i in range(PAIR):
            h = c * PAIR + i
            gq_v[:, h * HD : (h + 1) * HD] = gq_c[:, i * QBLK : (i + 1) * QBLK].T.astype(bf16)
        for r in range(1, kvh_count):
            gq_copy(c, r).start()

    v_t = v_all.astype(f32).T.astype(bf16)
    for c in range(chunks):
        at = slice(c * lanes, (c + 1) * lanes)
        att_c = dot(v_t, prob_half[:, at], NN)
        for i in range(PAIR):
            h = c * PAIR + i
            att_v[:, h * HD : (h + 1) * HD] = att_c[:, i * QBLK : (i + 1) * QBLK].T.astype(bf16)

    stores = [
        pltpu.make_async_copy(
            gq_v.at[pl.ds(pl.multiple_of(head * part, part), part), :],
            gq_out.at[:, pl.ds(pl.multiple_of(head * width, width), width)],
            store_sem.at[0],
        ),
        pltpu.make_async_copy(own, own_out, store_sem.at[1]),
        pltpu.make_async_copy(att_v, att_out, store_sem.at[2]),
        pltpu.make_async_copy(sel_in, sel_store, store_sem.at[3]),
    ]
    for copy in stores:
        copy.start()

    for j, d in enumerate(distances):

        @pl.when(me + d < ctx_count)
        def _(j=j, d=d):
            k_copy(j, d).wait_send()
            v_copy(j, d).wait_send()
            term_copy(1, j, d).wait_recv()
            term_copy(0, j, d).wait_recv()

        @pl.when(me - d >= 0)
        def _(j=j, d=d):
            sel_copy(j, d).wait_send()
            term_copy(1, j, d).wait_send()
            term_copy(0, j, d).wait_send()

    for c in range(chunks):
        for r in range(1, kvh_count):
            gq_copy(c, r).wait()
    for copy in stores:
        copy.wait()


def finish(ctx_count, distances, att, gq, own, terms, sel, att_hbm, gq_hbm, gk_hbm, gv_hbm, total, sem):
    me = lax.axis_index("ctx")
    stores = [
        pltpu.make_async_copy(src, dst, sem.at[i])
        for i, (src, dst) in enumerate(
            [(att, att_hbm), (gq, gq_hbm), (total.at[0], gk_hbm), (total.at[1], gv_hbm)]
        )
    ]
    stores[0].start()
    stores[1].start()
    for i in range(2):
        total[i, 0:KBLK] = own[i]
        total[i, KBLK : 2 * KBLK] = jnp.zeros((KBLK, HD), jnp.float32)
    for j, d in enumerate(distances):

        @pl.when(me + d < ctx_count)
        def _(j=j, d=d):
            where = jnp.broadcast_to(sel[j, 0:1], (KBLK, HD))
            for i in range(2):
                term = terms[i, j].astype(jnp.float32)
                total[i, 0:KBLK] += jnp.where(where == 0, term, 0.0)
                total[i, KBLK : 2 * KBLK] += jnp.where(where == 1, term, 0.0)

    stores[2].start()
    stores[3].start()
    for copy in stores:
        copy.wait()


def solution(mesh):
    ctx_count = mesh.shape["ctx"]
    kvh_count = mesh.shape["kvh"]
    distances = [1 << j for j in range(SLOTS - 1) if 1 << j < ctx_count]
    far = len(distances)
    slots = 1 + far

    def on_device(queries, keys, values, upstream, selected, counts):
        tokens, width = queries.shape
        key_rows = keys.shape[0]
        assert tokens == QBLK and key_rows == 2 * KBLK and selected.shape[0] == 1
        chunks = GROUP // PAIR
        bf16, f32 = jnp.bfloat16, jnp.float32
        dma = pltpu.SemaphoreType.DMA
        smem = pl.BlockSpec(memory_space=pltpu.SMEM)
        hbm = pl.BlockSpec(memory_space=pltpu.HBM)
        vmem = pl.BlockSpec(memory_space=pltpu.VMEM)
        anywhere = pl.BlockSpec(memory_space=pl.ANY)
        result = [
            jax.ShapeDtypeStruct((tokens, width), bf16),
            jax.ShapeDtypeStruct((tokens // kvh_count, width * kvh_count), bf16),
        ]
        grad = jax.ShapeDtypeStruct((key_rows, HD), f32)
        parts = pl.pallas_call(
            functools.partial(kernel, ctx_count, kvh_count, distances),
            out_shape=result
            + [
                jax.ShapeDtypeStruct((2, KBLK, HD), f32),
                jax.ShapeDtypeStruct((2, far, KBLK, HD), bf16),
                jax.ShapeDtypeStruct((far, 8, HD), jnp.int32),
            ],
            in_specs=[smem] + [hbm] * 5,
            out_specs=[anywhere] * 5,
            scratch_shapes=[
                pltpu.SMEM((1, SLOTS), jnp.int32),
                pltpu.VMEM((tokens, width), bf16),
                pltpu.VMEM((tokens, width), bf16),
                pltpu.VMEM((HD, GROUP * tokens), bf16),
                pltpu.VMEM((HD, GROUP * tokens), bf16),
                pltpu.VMEM((key_rows, HD), bf16),
                pltpu.VMEM((key_rows, HD), bf16),
                pltpu.VMEM((far, KBLK, HD), bf16),
                pltpu.VMEM((far, KBLK, HD), bf16),
                pltpu.VMEM((far, KBLK, HD), bf16),
                pltpu.VMEM((far, KBLK, HD), bf16),
                pltpu.VMEM((far, 8, HD), jnp.int32),
                pltpu.VMEM((far, 8, HD), jnp.int32),
                pltpu.VMEM((slots * KBLK, HD), bf16),
                pltpu.VMEM((slots * KBLK, HD), bf16),
                pltpu.VMEM((slots * KBLK, GROUP * tokens), f32),
                pltpu.VMEM((slots * KBLK, GROUP * tokens), bf16),
                pltpu.VMEM((slots * KBLK, GROUP * tokens), bf16),
                pltpu.VMEM((tokens, width), bf16),
                pltpu.VMEM((tokens, width), bf16),
                pltpu.VMEM((2, KBLK, HD), f32),
                pltpu.VMEM((2, far, KBLK, HD), bf16),
                dma((5,)),
                dma((4,)),
                dma((2, far)),
                dma((2, far)),
                dma((far,)),
                dma((far,)),
                dma((2, far)),
                dma((2, far)),
                dma((chunks, kvh_count - 1)),
                dma((chunks, kvh_count - 1)),
            ],
            compiler_params=pltpu.CompilerParams(
                collective_id=0, has_side_effects=True, vmem_limit_bytes=32 * 1024 * 1024
            ),
        )(
            counts,
            *[
                pltpu.with_memory_space_constraint(x, pltpu.HBM)
                for x in (selected, queries, keys, values, upstream)
            ],
        )
        return pl.pallas_call(
            functools.partial(finish, ctx_count, distances),
            out_shape=result + [grad, grad],
            in_specs=[anywhere, anywhere, vmem, vmem, vmem],
            out_specs=[hbm] * 4,
            scratch_shapes=[pltpu.VMEM((2, key_rows, HD), f32), dma((4,))],
            compiler_params=pltpu.CompilerParams(vmem_limit_bytes=4 * 1024 * 1024),
        )(*parts)

    placed = (
        P("ctx", "kvh"),
        P("ctx", "kvh"),
        P("ctx", "kvh"),
        P("ctx", "kvh"),
        P("ctx", None),
        P("ctx"),
    )
    return jax.shard_map(
        on_device,
        mesh=mesh,
        in_specs=placed,
        out_specs=(P("ctx", "kvh"), P(("ctx", "kvh"), None), P("ctx", "kvh"), P("ctx", "kvh")),
        check_vma=False,
    )
```

```python
import functools
import math

import jax
import jax.numpy as jnp
from jax import lax
from jax.experimental import pallas as pl
from jax.experimental.pallas import tpu as pltpu
from jax.sharding import PartitionSpec as P

HD = 128
GROUP = 8
KBLK = 64
QBLK = 128
SLOTS = 8
PAIR = 2

MESH = pl.DeviceIdType.MESH
LOG2E = math.log2(math.e)
NN = (((1,), (0,)), ((), ()))


def dot(a, b, dims):
    return lax.dot_general(a, b, dims, preferred_element_type=jnp.float32)


def kernel(
    ctx_count,
    kvh_count,
    distances,
    cnt_ref,
    sel_hbm,
    q_hbm,
    k_hbm,
    v_hbm,
    u_hbm,
    att_out,
    gq_out,
    own_out,
    terms_in,
    sel_store,
    sel_ref,
    q_v,
    u_v,
    q_t,
    u_t,
    k_own,
    v_own,
    k_out,
    v_out,
    k_in,
    v_in,
    sel_out,
    sel_in,
    keys,
    vals,
    prob,
    prob_half,
    grad_scores,
    att_v,
    gq_v,
    own,
    terms_out,
    load_sem,
    store_sem,
    kv_send,
    kv_recv,
    sel_send,
    sel_recv,
    term_send,
    term_recv,
    gq_send,
    gq_recv,
):
    score_scale = 1.0 / math.sqrt(HD)
    bf16, f32 = jnp.bfloat16, jnp.float32
    me = lax.axis_index("ctx")
    head = lax.axis_index("kvh")
    slots = 1 + len(distances)
    part = QBLK // kvh_count
    width = GROUP * HD
    chunks = GROUP // PAIR
    lanes = PAIR * QBLK

    loads = [
        pltpu.make_async_copy(src, dst, load_sem.at[i])
        for i, (src, dst) in enumerate(
            [
                (sel_hbm, sel_ref),
                (k_hbm, k_own),
                (v_hbm, v_own),
                (q_hbm, q_v),
                (u_hbm, u_v),
            ]
        )
    ]
    for copy in loads:
        copy.start()

    barrier = pltpu.get_barrier_semaphore()
    for r in range(1, kvh_count):
        peer = lax.rem(head + r, kvh_count)
        pl.semaphore_signal(barrier, inc=1, device_id={"kvh": peer}, device_id_type=MESH)
    for d in distances:

        @pl.when(me + d < ctx_count)
        def _():
            pl.semaphore_signal(barrier, inc=1, device_id={"ctx": me + d}, device_id_type=MESH)

        @pl.when(me - d >= 0)
        def _():
            pl.semaphore_signal(barrier, inc=1, device_id={"ctx": me - d}, device_id_type=MESH)

    for copy in loads[:3]:
        copy.wait()
    for j, d in enumerate(distances):
        sel_out[j] = jnp.full((8, HD), sel_ref[0, j + 1] - 2 * (me - d), jnp.int32)

    partners = kvh_count - 1
    for d in distances:
        partners += 1 - (me + d) // ctx_count + (me - d + ctx_count) // ctx_count
    pl.semaphore_wait(barrier, partners)

    def remote(src, dst, send, recv, **where):
        return pltpu.make_async_remote_copy(
            src_ref=src, dst_ref=dst, send_sem=send, recv_sem=recv,
            device_id=where, device_id_type=MESH,
        )

    def k_copy(j, d):
        return remote(k_out.at[j], k_in.at[j], kv_send.at[0, j], kv_recv.at[0, j], ctx=me + d)

    def v_copy(j, d):
        return remote(v_out.at[j], v_in.at[j], kv_send.at[1, j], kv_recv.at[1, j], ctx=me + d)

    def sel_copy(j, d):
        return remote(sel_out.at[j], sel_in.at[j], sel_send.at[j], sel_recv.at[j], ctx=me - d)

    def term_copy(i, j, d):
        return remote(
            terms_out.at[i, j], terms_in.at[i, j], term_send.at[i, j], term_recv.at[i, j], ctx=me - d
        )

    def gq_copy(c, r):
        cols = PAIR * HD
        peer = lax.rem(head + r, kvh_count)
        return remote(
            gq_v.at[pl.ds(pl.multiple_of(peer * part, part), part), pl.ds(pl.multiple_of(c * cols, cols), cols)],
            gq_out.at[:, pl.ds(pl.multiple_of(head * width + c * cols, cols), cols)],
            gq_send.at[c, r - 1],
            gq_recv.at[c, r - 1],
            kvh=peer,
        )

    by_far = list(enumerate(distances))[::-1]
    for j, d in by_far:

        @pl.when(me - d >= 0)
        def _(j=j, d=d):
            sel_copy(j, d).start()

    for copy in loads[3:]:
        copy.wait()

    def transpose(rows, columns):
        @pl.loop(0, GROUP)
        def _(h):
            at = pl.ds(pl.multiple_of(h * HD, HD), HD)
            columns[:, at] = rows[:, at].astype(f32).T.astype(bf16)

    def send_rows(make, own_rows, out, first):
        for j, d in enumerate(distances):

            @pl.when(me + d < ctx_count)
            def _(j=j, d=d):
                if first:
                    sel_copy(j, d).wait_recv()
                upper = jnp.broadcast_to(sel_in[j, 0:1], (KBLK, HD)) > 0
                lo = own_rows[0:KBLK].astype(f32)
                hi = own_rows[KBLK : 2 * KBLK].astype(f32)
                out[j] = jnp.where(upper, hi, lo).astype(bf16)
                make(j, d).start()

    transpose(q_v, q_t)
    send_rows(k_copy, k_own, k_out, True)
    send_rows(v_copy, v_own, v_out, False)
    transpose(u_v, u_t)

    count = cnt_ref[0]

    def receive(make, own_rows, arrived, chosen):
        chosen[0:KBLK] = own_rows[0:KBLK]
        for j, d in enumerate(distances):

            @pl.when(me - d >= 0)
            def _(j=j, d=d):
                make(j, d).wait_recv()

            live = jnp.full((KBLK, HD), count > j + 1)
            rows = jnp.where(live, arrived[j].astype(f32), 0.0)
            chosen[(j + 1) * KBLK : (j + 2) * KBLK] = rows.astype(bf16)
        return chosen[...]

    def send_terms(i, term):
        own[i] = term[0:KBLK]
        for j, d in by_far:
            terms_out[i, j] = term[(j + 1) * KBLK : (j + 2) * KBLK].astype(bf16)

            @pl.when(me - d >= 0)
            def _(j=j, d=d):
                term_copy(i, j, d).start()

    def chunk(c):
        return pl.ds(pl.multiple_of(c * lanes, lanes), lanes)

    def one_head(c, i):
        return pl.ds(pl.multiple_of((c * PAIR + i) * HD, HD), HD)

    def by_rows(ref):
        return jnp.concatenate([ref[:, h * HD : (h + 1) * HD] for h in range(GROUP)], axis=0)

    k_all = receive(k_copy, k_own, k_in, keys)
    key_at = lax.broadcasted_iota(jnp.int32, (KBLK, lanes), 0)
    query_at = lax.rem(lax.broadcasted_iota(jnp.int32, (KBLK, lanes), 1), QBLK)
    causal = key_at <= query_at
    hidden = [jnp.full((KBLK, lanes), count <= j) for j in range(1, slots)]

    @pl.loop(0, chunks)
    def _(c):
        at = chunk(c)
        s = dot(k_all, q_t[:, at], NN)
        s = jnp.concatenate(
            [jnp.where(causal, s[0:KBLK], -1e30)]
            + [
                jnp.where(hidden[j - 1], -1e30, s[j * KBLK : (j + 1) * KBLK])
                for j in range(1, slots)
            ],
            axis=0,
        )
        peak = jnp.max(s, axis=0, keepdims=True)
        e = jnp.exp2((s - peak) * (score_scale * LOG2E))
        p = e * (1.0 / jnp.sum(e, axis=0, keepdims=True))
        prob[:, at] = p
        prob_half[:, at] = p.astype(bf16)

    send_terms(1, dot(prob_half[...], by_rows(u_v), NN))

    v_all = receive(v_copy, v_own, v_in, vals)

    @pl.loop(0, chunks)
    def _(c):
        at = chunk(c)
        dp = dot(v_all, u_t[:, at], NN)
        p = prob[:, at]
        row_term = jnp.sum(p * dp, axis=0, keepdims=True)
        ds = (p * (dp - row_term)).astype(bf16)
        grad_scores[:, at] = ds

    send_terms(0, dot(grad_scores[...], by_rows(q_v), NN) * score_scale)

    k_t = k_all.astype(f32).T.astype(bf16)

    @pl.loop(0, chunks)
    def _(c):
        gq_c = dot(k_t, grad_scores[:, chunk(c)], NN) * score_scale
        for i in range(PAIR):
            gq_v[:, one_head(c, i)] = gq_c[:, i * QBLK : (i + 1) * QBLK].T.astype(bf16)
        for r in range(1, kvh_count):
            gq_copy(c, r).start()

    v_t = v_all.astype(f32).T.astype(bf16)

    @pl.loop(0, chunks)
    def _(c):
        att_c = dot(v_t, prob_half[:, chunk(c)], NN)
        for i in range(PAIR):
            att_v[:, one_head(c, i)] = att_c[:, i * QBLK : (i + 1) * QBLK].T.astype(bf16)

    stores = [
        pltpu.make_async_copy(
            gq_v.at[pl.ds(pl.multiple_of(head * part, part), part), :],
            gq_out.at[:, pl.ds(pl.multiple_of(head * width, width), width)],
            store_sem.at[0],
        ),
        pltpu.make_async_copy(own, own_out, store_sem.at[1]),
        pltpu.make_async_copy(att_v, att_out, store_sem.at[2]),
        pltpu.make_async_copy(sel_in, sel_store, store_sem.at[3]),
    ]
    for copy in stores:
        copy.start()

    for j, d in enumerate(distances):

        @pl.when(me + d < ctx_count)
        def _(j=j, d=d):
            k_copy(j, d).wait_send()
            v_copy(j, d).wait_send()
            term_copy(1, j, d).wait_recv()
            term_copy(0, j, d).wait_recv()

        @pl.when(me - d >= 0)
        def _(j=j, d=d):
            sel_copy(j, d).wait_send()
            term_copy(1, j, d).wait_send()
            term_copy(0, j, d).wait_send()

    for c in range(chunks):
        for r in range(1, kvh_count):
            gq_copy(c, r).wait()
    for copy in stores:
        copy.wait()


def finish(ctx_count, distances, att, gq, own, terms, sel, att_hbm, gq_hbm, gk_hbm, gv_hbm, total, sem):
    me = lax.axis_index("ctx")
    stores = [
        pltpu.make_async_copy(src, dst, sem.at[i])
        for i, (src, dst) in enumerate(
            [(att, att_hbm), (gq, gq_hbm), (total.at[0], gk_hbm), (total.at[1], gv_hbm)]
        )
    ]
    stores[0].start()
    stores[1].start()
    for i in range(2):
        total[i, 0:KBLK] = own[i]
        total[i, KBLK : 2 * KBLK] = jnp.zeros((KBLK, HD), jnp.float32)
    for j, d in enumerate(distances):

        @pl.when(me + d < ctx_count)
        def _(j=j, d=d):
            where = jnp.broadcast_to(sel[j, 0:1], (KBLK, HD))
            for i in range(2):
                term = terms[i, j].astype(jnp.float32)
                total[i, 0:KBLK] += jnp.where(where == 0, term, 0.0)
                total[i, KBLK : 2 * KBLK] += jnp.where(where == 1, term, 0.0)

    stores[2].start()
    stores[3].start()
    for copy in stores:
        copy.wait()


def solution(mesh):
    ctx_count = mesh.shape["ctx"]
    kvh_count = mesh.shape["kvh"]
    distances = [1 << j for j in range(SLOTS - 1) if 1 << j < ctx_count]
    far = len(distances)
    slots = 1 + far

    def on_device(queries, keys, values, upstream, selected, counts):
        tokens, width = queries.shape
        key_rows = keys.shape[0]
        assert tokens == QBLK and key_rows == 2 * KBLK and selected.shape[0] == 1
        chunks = GROUP // PAIR
        bf16, f32 = jnp.bfloat16, jnp.float32
        dma = pltpu.SemaphoreType.DMA
        smem = pl.BlockSpec(memory_space=pltpu.SMEM)
        hbm = pl.BlockSpec(memory_space=pltpu.HBM)
        vmem = pl.BlockSpec(memory_space=pltpu.VMEM)
        anywhere = pl.BlockSpec(memory_space=pl.ANY)
        result = [
            jax.ShapeDtypeStruct((tokens, width), bf16),
            jax.ShapeDtypeStruct((tokens // kvh_count, width * kvh_count), bf16),
        ]
        grad = jax.ShapeDtypeStruct((key_rows, HD), f32)
        parts = pl.pallas_call(
            functools.partial(kernel, ctx_count, kvh_count, distances),
            out_shape=result
            + [
                jax.ShapeDtypeStruct((2, KBLK, HD), f32),
                jax.ShapeDtypeStruct((2, far, KBLK, HD), bf16),
                jax.ShapeDtypeStruct((far, 8, HD), jnp.int32),
            ],
            in_specs=[smem] + [hbm] * 5,
            out_specs=[anywhere] * 5,
            scratch_shapes=[
                pltpu.SMEM((1, SLOTS), jnp.int32),
                pltpu.VMEM((tokens, width), bf16),
                pltpu.VMEM((tokens, width), bf16),
                pltpu.VMEM((HD, GROUP * tokens), bf16),
                pltpu.VMEM((HD, GROUP * tokens), bf16),
                pltpu.VMEM((key_rows, HD), bf16),
                pltpu.VMEM((key_rows, HD), bf16),
                pltpu.VMEM((far, KBLK, HD), bf16),
                pltpu.VMEM((far, KBLK, HD), bf16),
                pltpu.VMEM((far, KBLK, HD), bf16),
                pltpu.VMEM((far, KBLK, HD), bf16),
                pltpu.VMEM((far, 8, HD), jnp.int32),
                pltpu.VMEM((far, 8, HD), jnp.int32),
                pltpu.VMEM((slots * KBLK, HD), bf16),
                pltpu.VMEM((slots * KBLK, HD), bf16),
                pltpu.VMEM((slots * KBLK, GROUP * tokens), f32),
                pltpu.VMEM((slots * KBLK, GROUP * tokens), bf16),
                pltpu.VMEM((slots * KBLK, GROUP * tokens), bf16),
                pltpu.VMEM((tokens, width), bf16),
                pltpu.VMEM((tokens, width), bf16),
                pltpu.VMEM((2, KBLK, HD), f32),
                pltpu.VMEM((2, far, KBLK, HD), bf16),
                dma((5,)),
                dma((4,)),
                dma((2, far)),
                dma((2, far)),
                dma((far,)),
                dma((far,)),
                dma((2, far)),
                dma((2, far)),
                dma((chunks, kvh_count - 1)),
                dma((chunks, kvh_count - 1)),
            ],
            compiler_params=pltpu.CompilerParams(
                collective_id=0, has_side_effects=True, vmem_limit_bytes=32 * 1024 * 1024
            ),
        )(
            counts,
            *[
                pltpu.with_memory_space_constraint(x, pltpu.HBM)
                for x in (selected, queries, keys, values, upstream)
            ],
        )
        return pl.pallas_call(
            functools.partial(finish, ctx_count, distances),
            out_shape=result + [grad, grad],
            in_specs=[anywhere, anywhere, vmem, vmem, vmem],
            out_specs=[hbm] * 4,
            scratch_shapes=[pltpu.VMEM((2, key_rows, HD), f32), dma((4,))],
            compiler_params=pltpu.CompilerParams(vmem_limit_bytes=4 * 1024 * 1024),
        )(*parts)

    placed = (
        P("ctx", "kvh"),
        P("ctx", "kvh"),
        P("ctx", "kvh"),
        P("ctx", "kvh"),
        P("ctx", None),
        P("ctx"),
    )
    return jax.shard_map(
        on_device,
        mesh=mesh,
        in_specs=placed,
        out_specs=(P("ctx", "kvh"), P(("ctx", "kvh"), None), P("ctx", "kvh"), P("ctx", "kvh")),
        check_vma=False,
    )
```

```python
import functools
import math

import jax
import jax.numpy as jnp
from jax import lax
from jax.experimental import pallas as pl
from jax.experimental.pallas import tpu as pltpu
from jax.sharding import PartitionSpec as P

HD = 128
GROUP = 8
KBLK = 64
QBLK = 128
SLOTS = 8
PAIR = 2

MESH = pl.DeviceIdType.MESH
LOG2E = math.log2(math.e)
NN = (((1,), (0,)), ((), ()))
NT = (((1,), (1,)), ((), ()))


def dot(a, b, dims):
    return lax.dot_general(a, b, dims, preferred_element_type=jnp.float32)


def kernel(
    ctx_count,
    kvh_count,
    distances,
    cnt_ref,
    sel_hbm,
    q_hbm,
    k_hbm,
    v_hbm,
    u_hbm,
    att_out,
    gq_out,
    own_out,
    terms_in,
    sel_store,
    q_v,
    u_v,
    k_own,
    v_own,
    k_out,
    v_out,
    k_in,
    v_in,
    sel_in,
    keys,
    vals,
    prob,
    prob_half,
    grad_scores,
    att_v,
    gq_v,
    own,
    terms_out,
    load_sem,
    store_sem,
    kv_send,
    kv_recv,
    sel_send,
    sel_recv,
    term_send,
    term_recv,
    gq_send,
    gq_recv,
):
    score_scale = 1.0 / math.sqrt(HD)
    bf16, f32 = jnp.bfloat16, jnp.float32
    me = lax.axis_index("ctx")
    head = lax.axis_index("kvh")
    slots = 1 + len(distances)
    part = QBLK // kvh_count
    width = GROUP * HD
    chunks = GROUP // PAIR
    lanes = PAIR * QBLK

    loads = [
        pltpu.make_async_copy(src, dst, load_sem.at[i])
        for i, (src, dst) in enumerate(
            [
                (k_hbm, k_own),
                (v_hbm, v_own),
                (q_hbm, q_v),
                (u_hbm, u_v),
            ]
        )
    ]
    for copy in loads:
        copy.start()

    barrier = pltpu.get_barrier_semaphore()
    for r in range(1, kvh_count):
        peer = lax.rem(head + r, kvh_count)
        pl.semaphore_signal(barrier, inc=1, device_id={"kvh": peer}, device_id_type=MESH)
    for d in distances:

        @pl.when(me + d < ctx_count)
        def _():
            pl.semaphore_signal(barrier, inc=1, device_id={"ctx": me + d}, device_id_type=MESH)

        @pl.when(me - d >= 0)
        def _():
            pl.semaphore_signal(barrier, inc=1, device_id={"ctx": me - d}, device_id_type=MESH)

    partners = kvh_count - 1
    for d in distances:
        partners += 1 - (me + d) // ctx_count + (me - d + ctx_count) // ctx_count
    pl.semaphore_wait(barrier, partners)

    def remote(src, dst, send, recv, **where):
        return pltpu.make_async_remote_copy(
            src_ref=src, dst_ref=dst, send_sem=send, recv_sem=recv,
            device_id=where, device_id_type=MESH,
        )

    def k_copy(j, d):
        return remote(k_out.at[j], k_in.at[j], kv_send.at[0, j], kv_recv.at[0, j], ctx=me + d)

    def v_copy(j, d):
        return remote(v_out.at[j], v_in.at[j], kv_send.at[1, j], kv_recv.at[1, j], ctx=me + d)

    def sel_copy(j, d):
        return remote(sel_hbm, sel_in.at[j], sel_send.at[j], sel_recv.at[j], ctx=me - d)

    def term_copy(i, j, d):
        return remote(
            terms_out.at[i, j], terms_in.at[i, j], term_send.at[i, j], term_recv.at[i, j], ctx=me - d
        )

    def gq_copy(c, r):
        cols = PAIR * HD
        peer = lax.rem(head + r, kvh_count)
        return remote(
            gq_v.at[pl.ds(pl.multiple_of(peer * part, part), part), pl.ds(c * cols, cols)],
            gq_out.at[:, pl.ds(pl.multiple_of(head * width + c * cols, cols), cols)],
            gq_send.at[c, r - 1],
            gq_recv.at[c, r - 1],
            kvh=peer,
        )

    by_far = list(enumerate(distances))[::-1]
    for j, d in by_far:

        @pl.when(me - d >= 0)
        def _(j=j, d=d):
            sel_copy(j, d).start()

    for copy in loads:
        copy.wait()

    def send_rows(make, own_rows, out, first):
        for j, d in enumerate(distances):

            @pl.when(me + d < ctx_count)
            def _(j=j, d=d):
                if first:
                    sel_copy(j, d).wait_recv()
                upper = jnp.broadcast_to(sel_in[j, :, j + 1 : j + 2], (KBLK, HD)) > 2 * me
                lo = own_rows[0:KBLK].astype(f32)
                hi = own_rows[KBLK : 2 * KBLK].astype(f32)
                out[j] = jnp.where(upper, hi, lo).astype(bf16)
                make(j, d).start()

    send_rows(k_copy, k_own, k_out, True)
    send_rows(v_copy, v_own, v_out, False)

    count = cnt_ref[0]

    def receive(make, own_rows, arrived, chosen):
        chosen[0:KBLK] = own_rows[0:KBLK]
        for j, d in enumerate(distances):

            @pl.when(me - d >= 0)
            def _(j=j, d=d):
                make(j, d).wait_recv()

            live = jnp.full((KBLK, HD), count > j + 1)
            rows = jnp.where(live, arrived[j].astype(f32), 0.0)
            chosen[(j + 1) * KBLK : (j + 2) * KBLK] = rows.astype(bf16)
        return chosen[...]

    def send_terms(i, term):
        own[i] = term[0:KBLK]
        for j, d in by_far:
            terms_out[i, j] = term[(j + 1) * KBLK : (j + 2) * KBLK].astype(bf16)

            @pl.when(me - d >= 0)
            def _(j=j, d=d):
                term_copy(i, j, d).start()

    def by_rows(ref):
        return jnp.concatenate([ref[:, h * HD : (h + 1) * HD] for h in range(GROUP)], axis=0)

    q_rows = by_rows(q_v)
    u_rows = by_rows(u_v)

    k_all = receive(k_copy, k_own, k_in, keys)
    key_at = lax.broadcasted_iota(jnp.int32, (KBLK, lanes), 0)
    query_at = lax.rem(lax.broadcasted_iota(jnp.int32, (KBLK, lanes), 1), QBLK)
    causal = key_at <= query_at
    hidden = [jnp.full((KBLK, lanes), count <= j) for j in range(1, slots)]
    for c in range(chunks):
        at = slice(c * lanes, (c + 1) * lanes)
        s = dot(k_all, q_rows[at], NT)
        s = jnp.concatenate(
            [jnp.where(causal, s[0:KBLK], -1e30)]
            + [
                jnp.where(hidden[j - 1], -1e30, s[j * KBLK : (j + 1) * KBLK])
                for j in range(1, slots)
            ],
            axis=0,
        )
        peak = jnp.max(s, axis=0, keepdims=True)
        e = jnp.exp2((s - peak) * (score_scale * LOG2E))
        p = e * (1.0 / jnp.sum(e, axis=0, keepdims=True))
        prob[:, at] = p
        prob_half[:, at] = p.astype(bf16)
    send_terms(1, dot(prob_half[...], u_rows, NN))

    v_all = receive(v_copy, v_own, v_in, vals)
    for c in range(chunks):
        at = slice(c * lanes, (c + 1) * lanes)
        dp = dot(v_all, u_rows[at], NT)
        p = prob[:, at]
        row_term = jnp.sum(p * dp, axis=0, keepdims=True)
        ds = (p * (dp - row_term)).astype(bf16)
        grad_scores[:, at] = ds
    send_terms(0, dot(grad_scores[...], q_rows, NN) * score_scale)

    k_t = k_all.astype(f32).T.astype(bf16)
    for c in range(chunks):
        at = slice(c * lanes, (c + 1) * lanes)
        gq_c = dot(k_t, grad_scores[:, at], NN) * score_scale
        for i in range(PAIR):
            h = c * PAIR + i
            gq_v[:, h * HD : (h + 1) * HD] = gq_c[:, i * QBLK : (i + 1) * QBLK].T.astype(bf16)
        for r in range(1, kvh_count):
            gq_copy(c, r).start()

    v_t = v_all.astype(f32).T.astype(bf16)
    for c in range(chunks):
        at = slice(c * lanes, (c + 1) * lanes)
        att_c = dot(v_t, prob_half[:, at], NN)
        for i in range(PAIR):
            h = c * PAIR + i
            att_v[:, h * HD : (h + 1) * HD] = att_c[:, i * QBLK : (i + 1) * QBLK].T.astype(bf16)

    stores = [
        pltpu.make_async_copy(
            gq_v.at[pl.ds(pl.multiple_of(head * part, part), part), :],
            gq_out.at[:, pl.ds(pl.multiple_of(head * width, width), width)],
            store_sem.at[0],
        ),
        pltpu.make_async_copy(own, own_out, store_sem.at[1]),
        pltpu.make_async_copy(att_v, att_out, store_sem.at[2]),
        pltpu.make_async_copy(sel_in, sel_store, store_sem.at[3]),
    ]
    for copy in stores:
        copy.start()

    for j, d in enumerate(distances):

        @pl.when(me + d < ctx_count)
        def _(j=j, d=d):
            k_copy(j, d).wait_send()
            v_copy(j, d).wait_send()
            term_copy(1, j, d).wait_recv()
            term_copy(0, j, d).wait_recv()

        @pl.when(me - d >= 0)
        def _(j=j, d=d):
            sel_copy(j, d).wait_send()
            term_copy(1, j, d).wait_send()
            term_copy(0, j, d).wait_send()

    for c in range(chunks):
        for r in range(1, kvh_count):
            gq_copy(c, r).wait()
    for copy in stores:
        copy.wait()


def finish(ctx_count, distances, att, gq, own, terms, sel, att_hbm, gq_hbm, gk_hbm, gv_hbm, total, sem):
    me = lax.axis_index("ctx")
    stores = [
        pltpu.make_async_copy(src, dst, sem.at[i])
        for i, (src, dst) in enumerate(
            [(att, att_hbm), (gq, gq_hbm), (total.at[0], gk_hbm), (total.at[1], gv_hbm)]
        )
    ]
    stores[0].start()
    stores[1].start()
    for i in range(2):
        total[i, 0:KBLK] = own[i]
        total[i, KBLK : 2 * KBLK] = jnp.zeros((KBLK, HD), jnp.float32)
    for j, d in enumerate(distances):

        @pl.when(me + d < ctx_count)
        def _(j=j, d=d):
            where = jnp.broadcast_to(sel[j, :, j + 1 : j + 2], (KBLK, HD)) - 2 * me
            for i in range(2):
                term = terms[i, j].astype(jnp.float32)
                total[i, 0:KBLK] += jnp.where(where == 0, term, 0.0)
                total[i, KBLK : 2 * KBLK] += jnp.where(where == 1, term, 0.0)

    stores[2].start()
    stores[3].start()
    for copy in stores:
        copy.wait()


def solution(mesh):
    ctx_count = mesh.shape["ctx"]
    kvh_count = mesh.shape["kvh"]
    distances = [1 << j for j in range(SLOTS - 1) if 1 << j < ctx_count]
    far = len(distances)
    slots = 1 + far

    def on_device(queries, keys, values, upstream, selected, counts):
        tokens, width = queries.shape
        key_rows = keys.shape[0]
        assert tokens == QBLK and key_rows == 2 * KBLK and selected.shape[0] == 1
        chunks = GROUP // PAIR
        bf16, f32 = jnp.bfloat16, jnp.float32
        dma = pltpu.SemaphoreType.DMA
        smem = pl.BlockSpec(memory_space=pltpu.SMEM)
        hbm = pl.BlockSpec(memory_space=pltpu.HBM)
        vmem = pl.BlockSpec(memory_space=pltpu.VMEM)
        anywhere = pl.BlockSpec(memory_space=pl.ANY)
        result = [
            jax.ShapeDtypeStruct((tokens, width), bf16),
            jax.ShapeDtypeStruct((tokens // kvh_count, width * kvh_count), bf16),
        ]
        grad = jax.ShapeDtypeStruct((key_rows, HD), f32)
        parts = pl.pallas_call(
            functools.partial(kernel, ctx_count, kvh_count, distances),
            out_shape=result
            + [
                jax.ShapeDtypeStruct((2, KBLK, HD), f32),
                jax.ShapeDtypeStruct((2, far, KBLK, HD), bf16),
                jax.ShapeDtypeStruct((far, 1, SLOTS), jnp.int32),
            ],
            in_specs=[smem] + [hbm] * 5,
            out_specs=[anywhere] * 5,
            scratch_shapes=[
                pltpu.VMEM((tokens, width), bf16),
                pltpu.VMEM((tokens, width), bf16),
                pltpu.VMEM((key_rows, HD), bf16),
                pltpu.VMEM((key_rows, HD), bf16),
                pltpu.VMEM((far, KBLK, HD), bf16),
                pltpu.VMEM((far, KBLK, HD), bf16),
                pltpu.VMEM((far, KBLK, HD), bf16),
                pltpu.VMEM((far, KBLK, HD), bf16),
                pltpu.VMEM((far, 1, SLOTS), jnp.int32),
                pltpu.VMEM((slots * KBLK, HD), bf16),
                pltpu.VMEM((slots * KBLK, HD), bf16),
                pltpu.VMEM((slots * KBLK, GROUP * tokens), f32),
                pltpu.VMEM((slots * KBLK, GROUP * tokens), bf16),
                pltpu.VMEM((slots * KBLK, GROUP * tokens), bf16),
                pltpu.VMEM((tokens, width), bf16),
                pltpu.VMEM((tokens, width), bf16),
                pltpu.VMEM((2, KBLK, HD), f32),
                pltpu.VMEM((2, far, KBLK, HD), bf16),
                dma((4,)),
                dma((4,)),
                dma((2, far)),
                dma((2, far)),
                dma((far,)),
                dma((far,)),
                dma((2, far)),
                dma((2, far)),
                dma((chunks, kvh_count - 1)),
                dma((chunks, kvh_count - 1)),
            ],
            compiler_params=pltpu.CompilerParams(
                collective_id=0, has_side_effects=True, vmem_limit_bytes=32 * 1024 * 1024
            ),
        )(
            counts,
            *[
                pltpu.with_memory_space_constraint(x, pltpu.HBM)
                for x in (selected, queries, keys, values, upstream)
            ],
        )
        return pl.pallas_call(
            functools.partial(finish, ctx_count, distances),
            out_shape=result + [grad, grad],
            in_specs=[anywhere, anywhere, vmem, vmem, vmem],
            out_specs=[hbm] * 4,
            scratch_shapes=[pltpu.VMEM((2, key_rows, HD), f32), dma((4,))],
            compiler_params=pltpu.CompilerParams(vmem_limit_bytes=4 * 1024 * 1024),
        )(*parts)

    placed = (
        P("ctx", "kvh"),
        P("ctx", "kvh"),
        P("ctx", "kvh"),
        P("ctx", "kvh"),
        P("ctx", None),
        P("ctx"),
    )
    return jax.shard_map(
        on_device,
        mesh=mesh,
        in_specs=placed,
        out_specs=(P("ctx", "kvh"), P(("ctx", "kvh"), None), P("ctx", "kvh"), P("ctx", "kvh")),
        check_vma=False,
    )
```

```python
import functools
import math

import jax
import jax.numpy as jnp
from jax import lax
from jax.experimental import pallas as pl
from jax.experimental.pallas import tpu as pltpu
from jax.sharding import PartitionSpec as P

HD = 128
GROUP = 8
KBLK = 64
QBLK = 128
SLOTS = 8
PAIR = 2

MESH = pl.DeviceIdType.MESH
LOG2E = math.log2(math.e)
NN = (((1,), (0,)), ((), ()))
NT = (((1,), (1,)), ((), ()))


def dot(a, b, dims):
    return lax.dot_general(a, b, dims, preferred_element_type=jnp.float32)


def kernel(
    ctx_count,
    kvh_count,
    distances,
    cnt_ref,
    sel_hbm,
    q_hbm,
    k_hbm,
    v_hbm,
    u_hbm,
    att_out,
    gq_out,
    own_out,
    terms_in,
    sel_store,
    q_v,
    u_v,
    k_own,
    v_own,
    k_out,
    v_out,
    k_in,
    v_in,
    sel_in,
    keys,
    vals,
    expon,
    grad_probs,
    prob_half,
    grad_scores,
    att_v,
    gq_v,
    own,
    terms_out,
    load_sem,
    store_sem,
    kv_send,
    kv_recv,
    sel_send,
    sel_recv,
    term_send,
    term_recv,
    gq_send,
    gq_recv,
):
    score_scale = 1.0 / math.sqrt(HD)
    bf16, f32 = jnp.bfloat16, jnp.float32
    me = lax.axis_index("ctx")
    head = lax.axis_index("kvh")
    slots = 1 + len(distances)
    part = QBLK // kvh_count
    width = GROUP * HD
    chunks = GROUP // PAIR
    lanes = PAIR * QBLK

    loads = [
        pltpu.make_async_copy(src, dst, load_sem.at[i])
        for i, (src, dst) in enumerate(
            [
                (k_hbm, k_own),
                (v_hbm, v_own),
                (q_hbm, q_v),
                (u_hbm, u_v),
            ]
        )
    ]
    for copy in loads:
        copy.start()

    barrier = pltpu.get_barrier_semaphore()
    for r in range(1, kvh_count):
        peer = lax.rem(head + r, kvh_count)
        pl.semaphore_signal(barrier, inc=1, device_id={"kvh": peer}, device_id_type=MESH)
    for d in distances:

        @pl.when(me + d < ctx_count)
        def _():
            pl.semaphore_signal(barrier, inc=1, device_id={"ctx": me + d}, device_id_type=MESH)

        @pl.when(me - d >= 0)
        def _():
            pl.semaphore_signal(barrier, inc=1, device_id={"ctx": me - d}, device_id_type=MESH)

    partners = kvh_count - 1
    for d in distances:
        partners += 1 - (me + d) // ctx_count + (me - d + ctx_count) // ctx_count
    pl.semaphore_wait(barrier, partners)

    def remote(src, dst, send, recv, **where):
        return pltpu.make_async_remote_copy(
            src_ref=src, dst_ref=dst, send_sem=send, recv_sem=recv,
            device_id=where, device_id_type=MESH,
        )

    def k_copy(j, d):
        return remote(k_out.at[j], k_in.at[j], kv_send.at[0, j], kv_recv.at[0, j], ctx=me + d)

    def v_copy(j, d):
        return remote(v_out.at[j], v_in.at[j], kv_send.at[1, j], kv_recv.at[1, j], ctx=me + d)

    def sel_copy(j, d):
        return remote(sel_hbm, sel_in.at[j], sel_send.at[j], sel_recv.at[j], ctx=me - d)

    def term_copy(i, j, d):
        return remote(
            terms_out.at[i, j], terms_in.at[i, j], term_send.at[i, j], term_recv.at[i, j], ctx=me - d
        )

    def gq_copy(c, r):
        cols = PAIR * HD
        peer = lax.rem(head + r, kvh_count)
        return remote(
            gq_v.at[pl.ds(pl.multiple_of(peer * part, part), part), pl.ds(c * cols, cols)],
            gq_out.at[:, pl.ds(pl.multiple_of(head * width + c * cols, cols), cols)],
            gq_send.at[c, r - 1],
            gq_recv.at[c, r - 1],
            kvh=peer,
        )

    by_far = list(enumerate(distances))[::-1]
    for j, d in by_far:

        @pl.when(me - d >= 0)
        def _(j=j, d=d):
            sel_copy(j, d).start()

    for copy in loads:
        copy.wait()

    def send_rows(make, own_rows, out, first):
        for j, d in enumerate(distances):

            @pl.when(me + d < ctx_count)
            def _(j=j, d=d):
                if first:
                    sel_copy(j, d).wait_recv()
                upper = jnp.broadcast_to(sel_in[j, :, j + 1 : j + 2], (KBLK, HD)) > 2 * me
                lo = own_rows[0:KBLK].astype(f32)
                hi = own_rows[KBLK : 2 * KBLK].astype(f32)
                out[j] = jnp.where(upper, hi, lo).astype(bf16)
                make(j, d).start()

    count = cnt_ref[0]
    key_at = lax.broadcasted_iota(jnp.int32, (KBLK, lanes), 0)
    query_at = lax.rem(lax.broadcasted_iota(jnp.int32, (KBLK, lanes), 1), QBLK)
    causal = key_at <= query_at
    every = [(c, slice(c * lanes, (c + 1) * lanes)) for c in range(chunks)]

    def slot_rows(j):
        return slice(j * KBLK, (j + 1) * KBLK)

    def heads_of(ref, c):
        return jnp.concatenate(
            [ref[:, h * HD : (h + 1) * HD] for h in range(c * PAIR, (c + 1) * PAIR)], axis=0
        )

    def receive(j, make, arrived, chosen):
        d = distances[j - 1]

        @pl.when(me - d >= 0)
        def _():
            make(j - 1, d).wait_recv()

        live = jnp.full((KBLK, HD), count > j)
        rows = jnp.where(live, arrived[j - 1].astype(f32), 0.0)
        chosen[slot_rows(j)] = rows.astype(bf16)

    peaks, sums, dots = {}, {}, {}

    def slot_scores(j):
        rows = keys[slot_rows(j)]
        for c, at in every:
            s = dot(rows, heads_of(q_v, c), NT)
            if j == 0:
                s = jnp.where(causal, s, -1e30)
            peak = jnp.max(s, axis=0, keepdims=True)
            e = jnp.exp2((s - peak) * (score_scale * LOG2E))
            expon[slot_rows(j), at] = e
            sums[j, c] = jnp.sum(e, axis=0, keepdims=True)
            peaks[j, c] = peak
            if j > 0:
                peaks[j, c] = jnp.where(jnp.full((1, lanes), count > j), peak, -1e30)

    def slot_grads(j):
        rows = vals[slot_rows(j)]
        for c, at in every:
            dp = dot(rows, heads_of(u_v, c), NT)
            grad_probs[slot_rows(j), at] = dp
            dots[j, c] = jnp.sum(expon[slot_rows(j), at] * dp, axis=0, keepdims=True)

    keys[slot_rows(0)] = k_own[0:KBLK]
    vals[slot_rows(0)] = v_own[0:KBLK]
    slot_scores(0)
    send_rows(k_copy, k_own, k_out, True)
    send_rows(v_copy, v_own, v_out, False)

    def send_terms(i, term):
        own[i] = term[0:KBLK]
        for j, d in by_far:
            terms_out[i, j] = term[(j + 1) * KBLK : (j + 2) * KBLK].astype(bf16)

            @pl.when(me - d >= 0)
            def _(j=j, d=d):
                term_copy(i, j, d).start()

    def by_rows(ref):
        return jnp.concatenate([ref[:, h * HD : (h + 1) * HD] for h in range(GROUP)], axis=0)

    slot_grads(0)
    for j in range(1, slots):
        receive(j, k_copy, k_in, keys)
        slot_scores(j)

    shares = {}
    for c, at in every:
        peak = functools.reduce(jnp.maximum, [peaks[j, c] for j in range(slots)])
        scale = [
            jnp.exp2((peaks[j, c] - peak) * (score_scale * LOG2E)) for j in range(slots)
        ]
        inverse = 1.0 / sum(scale[j] * sums[j, c] for j in range(slots))
        for j in range(slots):
            shares[j, c] = scale[j] * inverse
            p = expon[slot_rows(j), at] * shares[j, c]
            prob_half[slot_rows(j), at] = p.astype(bf16)
    send_terms(1, dot(prob_half[...], by_rows(u_v), NN))

    for j in range(1, slots):
        receive(j, v_copy, v_in, vals)
        slot_grads(j)

    for c, at in every:
        row_term = sum(shares[j, c] * dots[j, c] for j in range(slots))
        for j in range(slots):
            p = expon[slot_rows(j), at] * shares[j, c]
            ds = p * (grad_probs[slot_rows(j), at] - row_term)
            grad_scores[slot_rows(j), at] = ds.astype(bf16)
    send_terms(0, dot(grad_scores[...], by_rows(q_v), NN) * score_scale)

    k_t = keys[...].astype(f32).T.astype(bf16)
    for c in range(chunks):
        at = slice(c * lanes, (c + 1) * lanes)
        gq_c = dot(k_t, grad_scores[:, at], NN) * score_scale
        for i in range(PAIR):
            h = c * PAIR + i
            gq_v[:, h * HD : (h + 1) * HD] = gq_c[:, i * QBLK : (i + 1) * QBLK].T.astype(bf16)
        for r in range(1, kvh_count):
            gq_copy(c, r).start()

    v_t = vals[...].astype(f32).T.astype(bf16)
    for c in range(chunks):
        at = slice(c * lanes, (c + 1) * lanes)
        att_c = dot(v_t, prob_half[:, at], NN)
        for i in range(PAIR):
            h = c * PAIR + i
            att_v[:, h * HD : (h + 1) * HD] = att_c[:, i * QBLK : (i + 1) * QBLK].T.astype(bf16)

    stores = [
        pltpu.make_async_copy(
            gq_v.at[pl.ds(pl.multiple_of(head * part, part), part), :],
            gq_out.at[:, pl.ds(pl.multiple_of(head * width, width), width)],
            store_sem.at[0],
        ),
        pltpu.make_async_copy(own, own_out, store_sem.at[1]),
        pltpu.make_async_copy(att_v, att_out, store_sem.at[2]),
        pltpu.make_async_copy(sel_in, sel_store, store_sem.at[3]),
    ]
    for copy in stores:
        copy.start()

    for j, d in enumerate(distances):

        @pl.when(me + d < ctx_count)
        def _(j=j, d=d):
            k_copy(j, d).wait_send()
            v_copy(j, d).wait_send()
            term_copy(1, j, d).wait_recv()
            term_copy(0, j, d).wait_recv()

        @pl.when(me - d >= 0)
        def _(j=j, d=d):
            sel_copy(j, d).wait_send()
            term_copy(1, j, d).wait_send()
            term_copy(0, j, d).wait_send()

    for c in range(chunks):
        for r in range(1, kvh_count):
            gq_copy(c, r).wait()
    for copy in stores:
        copy.wait()


def finish(ctx_count, distances, att, gq, own, terms, sel, att_hbm, gq_hbm, gk_hbm, gv_hbm, total, sem):
    me = lax.axis_index("ctx")
    stores = [
        pltpu.make_async_copy(src, dst, sem.at[i])
        for i, (src, dst) in enumerate(
            [(att, att_hbm), (gq, gq_hbm), (total.at[0], gk_hbm), (total.at[1], gv_hbm)]
        )
    ]
    stores[0].start()
    stores[1].start()
    for i in range(2):
        total[i, 0:KBLK] = own[i]
        total[i, KBLK : 2 * KBLK] = jnp.zeros((KBLK, HD), jnp.float32)
    for j, d in enumerate(distances):

        @pl.when(me + d < ctx_count)
        def _(j=j, d=d):
            where = jnp.broadcast_to(sel[j, :, j + 1 : j + 2], (KBLK, HD)) - 2 * me
            for i in range(2):
                term = terms[i, j].astype(jnp.float32)
                total[i, 0:KBLK] += jnp.where(where == 0, term, 0.0)
                total[i, KBLK : 2 * KBLK] += jnp.where(where == 1, term, 0.0)

    stores[2].start()
    stores[3].start()
    for copy in stores:
        copy.wait()


def solution(mesh):
    ctx_count = mesh.shape["ctx"]
    kvh_count = mesh.shape["kvh"]
    distances = [1 << j for j in range(SLOTS - 1) if 1 << j < ctx_count]
    far = len(distances)
    slots = 1 + far

    def on_device(queries, keys, values, upstream, selected, counts):
        tokens, width = queries.shape
        key_rows = keys.shape[0]
        assert tokens == QBLK and key_rows == 2 * KBLK and selected.shape[0] == 1
        chunks = GROUP // PAIR
        bf16, f32 = jnp.bfloat16, jnp.float32
        dma = pltpu.SemaphoreType.DMA
        smem = pl.BlockSpec(memory_space=pltpu.SMEM)
        hbm = pl.BlockSpec(memory_space=pltpu.HBM)
        vmem = pl.BlockSpec(memory_space=pltpu.VMEM)
        anywhere = pl.BlockSpec(memory_space=pl.ANY)
        result = [
            jax.ShapeDtypeStruct((tokens, width), bf16),
            jax.ShapeDtypeStruct((tokens // kvh_count, width * kvh_count), bf16),
        ]
        grad = jax.ShapeDtypeStruct((key_rows, HD), f32)
        parts = pl.pallas_call(
            functools.partial(kernel, ctx_count, kvh_count, distances),
            out_shape=result
            + [
                jax.ShapeDtypeStruct((2, KBLK, HD), f32),
                jax.ShapeDtypeStruct((2, far, KBLK, HD), bf16),
                jax.ShapeDtypeStruct((far, 1, SLOTS), jnp.int32),
            ],
            in_specs=[smem] + [hbm] * 5,
            out_specs=[anywhere] * 5,
            scratch_shapes=[
                pltpu.VMEM((tokens, width), bf16),
                pltpu.VMEM((tokens, width), bf16),
                pltpu.VMEM((key_rows, HD), bf16),
                pltpu.VMEM((key_rows, HD), bf16),
                pltpu.VMEM((far, KBLK, HD), bf16),
                pltpu.VMEM((far, KBLK, HD), bf16),
                pltpu.VMEM((far, KBLK, HD), bf16),
                pltpu.VMEM((far, KBLK, HD), bf16),
                pltpu.VMEM((far, 1, SLOTS), jnp.int32),
                pltpu.VMEM((slots * KBLK, HD), bf16),
                pltpu.VMEM((slots * KBLK, HD), bf16),
                pltpu.VMEM((slots * KBLK, GROUP * tokens), f32),
                pltpu.VMEM((slots * KBLK, GROUP * tokens), f32),
                pltpu.VMEM((slots * KBLK, GROUP * tokens), bf16),
                pltpu.VMEM((slots * KBLK, GROUP * tokens), bf16),
                pltpu.VMEM((tokens, width), bf16),
                pltpu.VMEM((tokens, width), bf16),
                pltpu.VMEM((2, KBLK, HD), f32),
                pltpu.VMEM((2, far, KBLK, HD), bf16),
                dma((4,)),
                dma((4,)),
                dma((2, far)),
                dma((2, far)),
                dma((far,)),
                dma((far,)),
                dma((2, far)),
                dma((2, far)),
                dma((chunks, kvh_count - 1)),
                dma((chunks, kvh_count - 1)),
            ],
            compiler_params=pltpu.CompilerParams(
                collective_id=0, has_side_effects=True, vmem_limit_bytes=32 * 1024 * 1024
            ),
        )(
            counts,
            *[
                pltpu.with_memory_space_constraint(x, pltpu.HBM)
                for x in (selected, queries, keys, values, upstream)
            ],
        )
        return pl.pallas_call(
            functools.partial(finish, ctx_count, distances),
            out_shape=result + [grad, grad],
            in_specs=[anywhere, anywhere, vmem, vmem, vmem],
            out_specs=[hbm] * 4,
            scratch_shapes=[pltpu.VMEM((2, key_rows, HD), f32), dma((4,))],
            compiler_params=pltpu.CompilerParams(vmem_limit_bytes=4 * 1024 * 1024),
        )(*parts)

    placed = (
        P("ctx", "kvh"),
        P("ctx", "kvh"),
        P("ctx", "kvh"),
        P("ctx", "kvh"),
        P("ctx", None),
        P("ctx"),
    )
    return jax.shard_map(
        on_device,
        mesh=mesh,
        in_specs=placed,
        out_specs=(P("ctx", "kvh"), P(("ctx", "kvh"), None), P("ctx", "kvh"), P("ctx", "kvh")),
        check_vma=False,
    )
```

```python
import functools
import math

import jax
import jax.numpy as jnp
from jax import lax
from jax.experimental import pallas as pl
from jax.experimental.pallas import tpu as pltpu
from jax.sharding import PartitionSpec as P

HD = 128
GROUP = 8
KBLK = 64
QBLK = 128
SLOTS = 8
PAIR = 2

MESH = pl.DeviceIdType.MESH
LOG2E = math.log2(math.e)
NN = (((1,), (0,)), ((), ()))
NT = (((1,), (1,)), ((), ()))


def dot(a, b, dims):
    return lax.dot_general(a, b, dims, preferred_element_type=jnp.float32)


def kernel(
    ctx_count,
    kvh_count,
    distances,
    cnt_ref,
    sel_hbm,
    q_hbm,
    k_hbm,
    v_hbm,
    u_hbm,
    att_out,
    gq_out,
    own_out,
    terms_in,
    sel_store,
    q_v,
    u_v,
    k_own,
    v_own,
    k_out,
    v_out,
    k_in,
    v_in,
    sel_in,
    keys,
    vals,
    expon,
    grad_probs,
    prob_half,
    grad_scores,
    att_v,
    gq_v,
    own,
    terms_out,
    load_sem,
    store_sem,
    kv_send,
    kv_recv,
    sel_send,
    sel_recv,
    term_send,
    term_recv,
    gq_send,
    gq_recv,
):
    score_scale = 1.0 / math.sqrt(HD)
    bf16, f32 = jnp.bfloat16, jnp.float32
    me = lax.axis_index("ctx")
    head = lax.axis_index("kvh")
    slots = 1 + len(distances)
    part = QBLK // kvh_count
    width = GROUP * HD
    chunks = GROUP // PAIR
    lanes = PAIR * QBLK

    loads = [
        pltpu.make_async_copy(src, dst, load_sem.at[i])
        for i, (src, dst) in enumerate(
            [
                (k_hbm, k_own),
                (v_hbm, v_own),
                (q_hbm, q_v),
                (u_hbm, u_v),
            ]
        )
    ]
    for copy in loads:
        copy.start()

    barrier = pltpu.get_barrier_semaphore()
    for r in range(1, kvh_count):
        peer = lax.rem(head + r, kvh_count)
        pl.semaphore_signal(barrier, inc=1, device_id={"kvh": peer}, device_id_type=MESH)
    for d in distances:

        @pl.when(me + d < ctx_count)
        def _():
            pl.semaphore_signal(barrier, inc=1, device_id={"ctx": me + d}, device_id_type=MESH)

        @pl.when(me - d >= 0)
        def _():
            pl.semaphore_signal(barrier, inc=1, device_id={"ctx": me - d}, device_id_type=MESH)

    partners = kvh_count - 1
    for d in distances:
        partners += 1 - (me + d) // ctx_count + (me - d + ctx_count) // ctx_count
    pl.semaphore_wait(barrier, partners)

    def remote(src, dst, send, recv, **where):
        return pltpu.make_async_remote_copy(
            src_ref=src, dst_ref=dst, send_sem=send, recv_sem=recv,
            device_id=where, device_id_type=MESH,
        )

    def k_copy(j, d):
        return remote(k_out.at[j], k_in.at[j], kv_send.at[0, j], kv_recv.at[0, j], ctx=me + d)

    def v_copy(j, d):
        return remote(v_out.at[j], v_in.at[j], kv_send.at[1, j], kv_recv.at[1, j], ctx=me + d)

    def sel_copy(j, d):
        return remote(sel_hbm, sel_in.at[j], sel_send.at[j], sel_recv.at[j], ctx=me - d)

    def term_copy(i, j, d):
        return remote(
            terms_out.at[i, j], terms_in.at[i, j], term_send.at[i, j], term_recv.at[i, j], ctx=me - d
        )

    def gq_copy(c, r):
        cols = PAIR * HD
        peer = lax.rem(head + r, kvh_count)
        return remote(
            gq_v.at[pl.ds(pl.multiple_of(peer * part, part), part), pl.ds(c * cols, cols)],
            gq_out.at[:, pl.ds(pl.multiple_of(head * width + c * cols, cols), cols)],
            gq_send.at[c, r - 1],
            gq_recv.at[c, r - 1],
            kvh=peer,
        )

    by_far = list(enumerate(distances))[::-1]
    for j, d in by_far:

        @pl.when(me - d >= 0)
        def _(j=j, d=d):
            sel_copy(j, d).start()

    for copy in loads:
        copy.wait()

    def send_rows(make, own_rows, out, first):
        for j, d in enumerate(distances):

            @pl.when(me + d < ctx_count)
            def _(j=j, d=d):
                if first:
                    sel_copy(j, d).wait_recv()
                upper = jnp.broadcast_to(sel_in[j, :, j + 1 : j + 2], (KBLK, HD)) > 2 * me
                lo = own_rows[0:KBLK].astype(f32)
                hi = own_rows[KBLK : 2 * KBLK].astype(f32)
                out[j] = jnp.where(upper, hi, lo).astype(bf16)
                make(j, d).start()

    count = cnt_ref[0]
    key_at = lax.broadcasted_iota(jnp.int32, (KBLK, lanes), 0)
    query_at = lax.rem(lax.broadcasted_iota(jnp.int32, (KBLK, lanes), 1), QBLK)
    causal = key_at <= query_at
    every = [(c, slice(c * lanes, (c + 1) * lanes)) for c in range(chunks)]

    def slot_rows(j):
        return slice(j * KBLK, (j + 1) * KBLK)

    def heads_of(ref, c):
        return jnp.concatenate(
            [ref[:, h * HD : (h + 1) * HD] for h in range(c * PAIR, (c + 1) * PAIR)], axis=0
        )

    def receive(j, make, arrived, chosen):
        d = distances[j - 1]

        @pl.when(me - d >= 0)
        def _():
            make(j - 1, d).wait_recv()

        live = jnp.full((KBLK, HD), count > j)
        rows = jnp.where(live, arrived[j - 1].astype(f32), 0.0)
        chosen[slot_rows(j)] = rows.astype(bf16)

    peaks, sums, dots = {}, {}, {}

    def slot_scores(j):
        rows = keys[slot_rows(j)]
        for c, at in every:
            s = dot(rows, heads_of(q_v, c), NT)
            if j == 0:
                s = jnp.where(causal, s, -1e30)
            peak = jnp.max(s, axis=0, keepdims=True)
            e = jnp.exp2((s - peak) * (score_scale * LOG2E))
            expon[slot_rows(j), at] = e
            sums[j, c] = jnp.sum(e, axis=0, keepdims=True)
            peaks[j, c] = peak
            if j > 0:
                peaks[j, c] = jnp.where(jnp.full((1, lanes), count > j), peak, -1e30)

    def slot_grads(j):
        rows = vals[slot_rows(j)]
        for c, at in every:
            dp = dot(rows, heads_of(u_v, c), NT)
            grad_probs[slot_rows(j), at] = dp
            dots[j, c] = jnp.sum(expon[slot_rows(j), at] * dp, axis=0, keepdims=True)

    keys[slot_rows(0)] = k_own[0:KBLK]
    vals[slot_rows(0)] = v_own[0:KBLK]
    send_rows(k_copy, k_own, k_out, True)
    send_rows(v_copy, v_own, v_out, False)

    def send_terms(i, term):
        own[i] = term[0:KBLK]
        for j, d in by_far:
            terms_out[i, j] = term[(j + 1) * KBLK : (j + 2) * KBLK].astype(bf16)

            @pl.when(me - d >= 0)
            def _(j=j, d=d):
                term_copy(i, j, d).start()

    def by_rows(ref):
        return jnp.concatenate([ref[:, h * HD : (h + 1) * HD] for h in range(GROUP)], axis=0)

    slot_scores(0)
    slot_grads(0)
    for j in range(1, slots):
        receive(j, k_copy, k_in, keys)
        slot_scores(j)

    shares = {}
    for c, at in every:
        peak = functools.reduce(jnp.maximum, [peaks[j, c] for j in range(slots)])
        scale = [
            jnp.exp2((peaks[j, c] - peak) * (score_scale * LOG2E)) for j in range(slots)
        ]
        inverse = 1.0 / sum(scale[j] * sums[j, c] for j in range(slots))
        for j in range(slots):
            shares[j, c] = scale[j] * inverse
            p = expon[slot_rows(j), at] * shares[j, c]
            prob_half[slot_rows(j), at] = p.astype(bf16)
    send_terms(1, dot(prob_half[...], by_rows(u_v), NN))

    for j in range(1, slots):
        receive(j, v_copy, v_in, vals)
        slot_grads(j)

    k_t = keys[...].astype(f32).T.astype(bf16)

    def score_gradients(c, at):
        row_term = sum(shares[j, c] * dots[j, c] for j in range(slots))
        for j in range(slots):
            p = expon[slot_rows(j), at] * shares[j, c]
            ds = p * (grad_probs[slot_rows(j), at] - row_term)
            grad_scores[slot_rows(j), at] = ds.astype(bf16)

    def query_gradients(c, at):
        gq_c = dot(k_t, grad_scores[:, at], NN) * score_scale
        for i in range(PAIR):
            h = c * PAIR + i
            gq_v[:, h * HD : (h + 1) * HD] = gq_c[:, i * QBLK : (i + 1) * QBLK].T.astype(bf16)
        for r in range(1, kvh_count):
            gq_copy(c, r).start()

    score_gradients(*every[0])
    query_gradients(*every[0])
    for c, at in every[1:]:
        score_gradients(c, at)
    send_terms(0, dot(grad_scores[...], by_rows(q_v), NN) * score_scale)
    for c, at in every[1:]:
        query_gradients(c, at)

    v_t = vals[...].astype(f32).T.astype(bf16)
    for c in range(chunks):
        at = slice(c * lanes, (c + 1) * lanes)
        att_c = dot(v_t, prob_half[:, at], NN)
        for i in range(PAIR):
            h = c * PAIR + i
            att_v[:, h * HD : (h + 1) * HD] = att_c[:, i * QBLK : (i + 1) * QBLK].T.astype(bf16)

    stores = [
        pltpu.make_async_copy(
            gq_v.at[pl.ds(pl.multiple_of(head * part, part), part), :],
            gq_out.at[:, pl.ds(pl.multiple_of(head * width, width), width)],
            store_sem.at[0],
        ),
        pltpu.make_async_copy(own, own_out, store_sem.at[1]),
        pltpu.make_async_copy(att_v, att_out, store_sem.at[2]),
        pltpu.make_async_copy(sel_in, sel_store, store_sem.at[3]),
    ]
    for copy in stores:
        copy.start()

    for j, d in enumerate(distances):

        @pl.when(me + d < ctx_count)
        def _(j=j, d=d):
            k_copy(j, d).wait_send()
            v_copy(j, d).wait_send()
            term_copy(1, j, d).wait_recv()
            term_copy(0, j, d).wait_recv()

        @pl.when(me - d >= 0)
        def _(j=j, d=d):
            sel_copy(j, d).wait_send()
            term_copy(1, j, d).wait_send()
            term_copy(0, j, d).wait_send()

    for c in range(chunks):
        for r in range(1, kvh_count):
            gq_copy(c, r).wait()
    for copy in stores:
        copy.wait()


def finish(ctx_count, distances, att, gq, own, terms, sel, att_hbm, gq_hbm, gk_hbm, gv_hbm, total, sem):
    me = lax.axis_index("ctx")
    stores = [
        pltpu.make_async_copy(src, dst, sem.at[i])
        for i, (src, dst) in enumerate(
            [(att, att_hbm), (gq, gq_hbm), (total.at[0], gk_hbm), (total.at[1], gv_hbm)]
        )
    ]
    stores[0].start()
    stores[1].start()
    for i in range(2):
        total[i, 0:KBLK] = own[i]
        total[i, KBLK : 2 * KBLK] = jnp.zeros((KBLK, HD), jnp.float32)
    for j, d in enumerate(distances):

        @pl.when(me + d < ctx_count)
        def _(j=j, d=d):
            where = jnp.broadcast_to(sel[j, :, j + 1 : j + 2], (KBLK, HD)) - 2 * me
            for i in range(2):
                term = terms[i, j].astype(jnp.float32)
                total[i, 0:KBLK] += jnp.where(where == 0, term, 0.0)
                total[i, KBLK : 2 * KBLK] += jnp.where(where == 1, term, 0.0)

    stores[2].start()
    stores[3].start()
    for copy in stores:
        copy.wait()


def solution(mesh):
    ctx_count = mesh.shape["ctx"]
    kvh_count = mesh.shape["kvh"]
    distances = [1 << j for j in range(SLOTS - 1) if 1 << j < ctx_count]
    far = len(distances)
    slots = 1 + far

    def on_device(queries, keys, values, upstream, selected, counts):
        tokens, width = queries.shape
        key_rows = keys.shape[0]
        assert tokens == QBLK and key_rows == 2 * KBLK and selected.shape[0] == 1
        chunks = GROUP // PAIR
        bf16, f32 = jnp.bfloat16, jnp.float32
        dma = pltpu.SemaphoreType.DMA
        smem = pl.BlockSpec(memory_space=pltpu.SMEM)
        hbm = pl.BlockSpec(memory_space=pltpu.HBM)
        vmem = pl.BlockSpec(memory_space=pltpu.VMEM)
        anywhere = pl.BlockSpec(memory_space=pl.ANY)
        result = [
            jax.ShapeDtypeStruct((tokens, width), bf16),
            jax.ShapeDtypeStruct((tokens // kvh_count, width * kvh_count), bf16),
        ]
        grad = jax.ShapeDtypeStruct((key_rows, HD), f32)
        parts = pl.pallas_call(
            functools.partial(kernel, ctx_count, kvh_count, distances),
            out_shape=result
            + [
                jax.ShapeDtypeStruct((2, KBLK, HD), f32),
                jax.ShapeDtypeStruct((2, far, KBLK, HD), bf16),
                jax.ShapeDtypeStruct((far, 1, SLOTS), jnp.int32),
            ],
            in_specs=[smem] + [hbm] * 5,
            out_specs=[anywhere] * 5,
            scratch_shapes=[
                pltpu.VMEM((tokens, width), bf16),
                pltpu.VMEM((tokens, width), bf16),
                pltpu.VMEM((key_rows, HD), bf16),
                pltpu.VMEM((key_rows, HD), bf16),
                pltpu.VMEM((far, KBLK, HD), bf16),
                pltpu.VMEM((far, KBLK, HD), bf16),
                pltpu.VMEM((far, KBLK, HD), bf16),
                pltpu.VMEM((far, KBLK, HD), bf16),
                pltpu.VMEM((far, 1, SLOTS), jnp.int32),
                pltpu.VMEM((slots * KBLK, HD), bf16),
                pltpu.VMEM((slots * KBLK, HD), bf16),
                pltpu.VMEM((slots * KBLK, GROUP * tokens), f32),
                pltpu.VMEM((slots * KBLK, GROUP * tokens), f32),
                pltpu.VMEM((slots * KBLK, GROUP * tokens), bf16),
                pltpu.VMEM((slots * KBLK, GROUP * tokens), bf16),
                pltpu.VMEM((tokens, width), bf16),
                pltpu.VMEM((tokens, width), bf16),
                pltpu.VMEM((2, KBLK, HD), f32),
                pltpu.VMEM((2, far, KBLK, HD), bf16),
                dma((4,)),
                dma((4,)),
                dma((2, far)),
                dma((2, far)),
                dma((far,)),
                dma((far,)),
                dma((2, far)),
                dma((2, far)),
                dma((chunks, kvh_count - 1)),
                dma((chunks, kvh_count - 1)),
            ],
            compiler_params=pltpu.CompilerParams(
                collective_id=0, has_side_effects=True, vmem_limit_bytes=32 * 1024 * 1024
            ),
        )(
            counts,
            *[
                pltpu.with_memory_space_constraint(x, pltpu.HBM)
                for x in (selected, queries, keys, values, upstream)
            ],
        )
        return pl.pallas_call(
            functools.partial(finish, ctx_count, distances),
            out_shape=result + [grad, grad],
            in_specs=[anywhere, anywhere, vmem, vmem, vmem],
            out_specs=[hbm] * 4,
            scratch_shapes=[pltpu.VMEM((2, key_rows, HD), f32), dma((4,))],
            compiler_params=pltpu.CompilerParams(vmem_limit_bytes=4 * 1024 * 1024),
        )(*parts)

    placed = (
        P("ctx", "kvh"),
        P("ctx", "kvh"),
        P("ctx", "kvh"),
        P("ctx", "kvh"),
        P("ctx", None),
        P("ctx"),
    )
    return jax.shard_map(
        on_device,
        mesh=mesh,
        in_specs=placed,
        out_specs=(P("ctx", "kvh"), P(("ctx", "kvh"), None), P("ctx", "kvh"), P("ctx", "kvh")),
        check_vma=False,
    )
```

```python
import functools
import math

import jax
import jax.numpy as jnp
from jax import lax
from jax.experimental import pallas as pl
from jax.experimental.pallas import tpu as pltpu
from jax.sharding import PartitionSpec as P

HD = 128
GROUP = 8
KBLK = 64
QBLK = 128
SLOTS = 8
PAIR = 2
SENDS = 2

MESH = pl.DeviceIdType.MESH
LOG2E = math.log2(math.e)
NN = (((1,), (0,)), ((), ()))
NT = (((1,), (1,)), ((), ()))


def dot(a, b, dims):
    return lax.dot_general(a, b, dims, preferred_element_type=jnp.float32)


def kernel(
    ctx_count,
    kvh_count,
    distances,
    cnt_ref,
    sel_hbm,
    q_hbm,
    k_hbm,
    v_hbm,
    u_hbm,
    att_out,
    gq_out,
    own_out,
    terms_in,
    sel_store,
    q_v,
    u_v,
    k_own,
    v_own,
    kv_out,
    kv_in,
    sel_in,
    keys,
    vals,
    prob,
    prob_half,
    grad_scores,
    att_v,
    gq_v,
    own,
    terms_out,
    load_sem,
    store_sem,
    kv_send,
    kv_recv,
    sel_send,
    sel_recv,
    term_send,
    term_recv,
    gq_send,
    gq_recv,
):
    score_scale = 1.0 / math.sqrt(HD)
    bf16, f32 = jnp.bfloat16, jnp.float32
    me = lax.axis_index("ctx")
    head = lax.axis_index("kvh")
    slots = 1 + len(distances)
    part = QBLK // kvh_count
    width = GROUP * HD
    chunks = GROUP // PAIR
    lanes = PAIR * QBLK

    loads = [
        pltpu.make_async_copy(src, dst, load_sem.at[i])
        for i, (src, dst) in enumerate(
            [
                (k_hbm, k_own),
                (v_hbm, v_own),
                (q_hbm, q_v),
                (u_hbm, u_v),
            ]
        )
    ]
    for copy in loads:
        copy.start()

    barrier = pltpu.get_barrier_semaphore()
    for r in range(1, kvh_count):
        peer = lax.rem(head + r, kvh_count)
        pl.semaphore_signal(barrier, inc=1, device_id={"kvh": peer}, device_id_type=MESH)
    for d in distances:

        @pl.when(me + d < ctx_count)
        def _():
            pl.semaphore_signal(barrier, inc=1, device_id={"ctx": me + d}, device_id_type=MESH)

        @pl.when(me - d >= 0)
        def _():
            pl.semaphore_signal(barrier, inc=1, device_id={"ctx": me - d}, device_id_type=MESH)

    partners = kvh_count - 1
    for d in distances:
        partners += 1 - (me + d) // ctx_count + (me - d + ctx_count) // ctx_count
    pl.semaphore_wait(barrier, partners)

    def remote(src, dst, send, recv, **where):
        return pltpu.make_async_remote_copy(
            src_ref=src, dst_ref=dst, send_sem=send, recv_sem=recv,
            device_id=where, device_id_type=MESH,
        )

    def kv_copy(j, d):
        return remote(kv_out.at[j], kv_in.at[j], kv_send.at[j], kv_recv.at[j], ctx=me + d)

    def sel_copy(j, d):
        return remote(sel_hbm, sel_in.at[j], sel_send.at[j], sel_recv.at[j], ctx=me - d)

    def term_copy(i, j, d):
        return remote(
            terms_out.at[i, j], terms_in.at[i, j], term_send.at[i, j], term_recv.at[i, j], ctx=me - d
        )

    def gq_copy(c, r):
        cols = width // SENDS
        peer = lax.rem(head + r, kvh_count)
        return remote(
            gq_v.at[pl.ds(pl.multiple_of(peer * part, part), part), pl.ds(c * cols, cols)],
            gq_out.at[:, pl.ds(pl.multiple_of(head * width + c * cols, cols), cols)],
            gq_send.at[c, r - 1],
            gq_recv.at[c, r - 1],
            kvh=peer,
        )

    by_far = list(enumerate(distances))[::-1]
    for j, d in by_far:

        @pl.when(me - d >= 0)
        def _(j=j, d=d):
            sel_copy(j, d).start()

    for copy in loads:
        copy.wait()

    for j, d in enumerate(distances):

        @pl.when(me + d < ctx_count)
        def _(j=j, d=d):
            sel_copy(j, d).wait_recv()
            upper = jnp.broadcast_to(sel_in[j, :, j + 1 : j + 2], (KBLK, HD)) > 2 * me
            for i, own_rows in enumerate((k_own, v_own)):
                lo = own_rows[0:KBLK].astype(f32)
                hi = own_rows[KBLK : 2 * KBLK].astype(f32)
                kv_out[j, i * KBLK : (i + 1) * KBLK] = jnp.where(upper, hi, lo).astype(bf16)
            kv_copy(j, d).start()

    count = cnt_ref[0]

    def send_terms(i, term):
        own[i] = term[0:KBLK]
        for j, d in by_far:
            terms_out[i, j] = term[(j + 1) * KBLK : (j + 2) * KBLK].astype(bf16)

            @pl.when(me - d >= 0)
            def _(j=j, d=d):
                term_copy(i, j, d).start()

    def by_rows(ref):
        return jnp.concatenate([ref[:, h * HD : (h + 1) * HD] for h in range(GROUP)], axis=0)

    q_rows = by_rows(q_v)
    u_rows = by_rows(u_v)

    keys[0:KBLK] = k_own[0:KBLK]
    vals[0:KBLK] = v_own[0:KBLK]
    for j, d in enumerate(distances):

        @pl.when(me - d >= 0)
        def _(j=j, d=d):
            kv_copy(j, d).wait_recv()

        live = jnp.full((KBLK, HD), count > j + 1)
        for i, chosen in enumerate((keys, vals)):
            rows = kv_in[j, i * KBLK : (i + 1) * KBLK].astype(f32)
            chosen[(j + 1) * KBLK : (j + 2) * KBLK] = jnp.where(live, rows, 0.0).astype(bf16)
    k_all = keys[...]
    v_all = vals[...]
    key_at = lax.broadcasted_iota(jnp.int32, (KBLK, lanes), 0)
    query_at = lax.rem(lax.broadcasted_iota(jnp.int32, (KBLK, lanes), 1), QBLK)
    causal = key_at <= query_at
    hidden = [jnp.full((KBLK, lanes), count <= j) for j in range(1, slots)]
    for c in range(chunks):
        at = slice(c * lanes, (c + 1) * lanes)
        s = dot(k_all, q_rows[at], NT)
        s = jnp.concatenate(
            [jnp.where(causal, s[0:KBLK], -1e30)]
            + [
                jnp.where(hidden[j - 1], -1e30, s[j * KBLK : (j + 1) * KBLK])
                for j in range(1, slots)
            ],
            axis=0,
        )
        peak = jnp.max(s, axis=0, keepdims=True)
        e = jnp.exp2((s - peak) * (score_scale * LOG2E))
        p = e * (1.0 / jnp.sum(e, axis=0, keepdims=True))
        prob[:, at] = p
        prob_half[:, at] = p.astype(bf16)
    send_terms(1, dot(prob_half[...], u_rows, NN))

    for c in range(chunks):
        at = slice(c * lanes, (c + 1) * lanes)
        dp = dot(v_all, u_rows[at], NT)
        p = prob[:, at]
        row_term = jnp.sum(p * dp, axis=0, keepdims=True)
        ds = (p * (dp - row_term)).astype(bf16)
        grad_scores[:, at] = ds
    send_terms(0, dot(grad_scores[...], q_rows, NN) * score_scale)

    k_t = k_all.astype(f32).T.astype(bf16)
    for c in range(chunks):
        at = slice(c * lanes, (c + 1) * lanes)
        gq_c = dot(k_t, grad_scores[:, at], NN) * score_scale
        for i in range(PAIR):
            h = c * PAIR + i
            gq_v[:, h * HD : (h + 1) * HD] = gq_c[:, i * QBLK : (i + 1) * QBLK].T.astype(bf16)
        if (c + 1) * SENDS % chunks == 0:
            for r in range(1, kvh_count):
                gq_copy((c + 1) * SENDS // chunks - 1, r).start()

    v_t = v_all.astype(f32).T.astype(bf16)
    for c in range(chunks):
        at = slice(c * lanes, (c + 1) * lanes)
        att_c = dot(v_t, prob_half[:, at], NN)
        for i in range(PAIR):
            h = c * PAIR + i
            att_v[:, h * HD : (h + 1) * HD] = att_c[:, i * QBLK : (i + 1) * QBLK].T.astype(bf16)

    stores = [
        pltpu.make_async_copy(
            gq_v.at[pl.ds(pl.multiple_of(head * part, part), part), :],
            gq_out.at[:, pl.ds(pl.multiple_of(head * width, width), width)],
            store_sem.at[0],
        ),
        pltpu.make_async_copy(own, own_out, store_sem.at[1]),
        pltpu.make_async_copy(att_v, att_out, store_sem.at[2]),
        pltpu.make_async_copy(sel_in, sel_store, store_sem.at[3]),
    ]
    for copy in stores:
        copy.start()

    for j, d in enumerate(distances):

        @pl.when(me + d < ctx_count)
        def _(j=j, d=d):
            kv_copy(j, d).wait_send()
            term_copy(1, j, d).wait_recv()
            term_copy(0, j, d).wait_recv()

        @pl.when(me - d >= 0)
        def _(j=j, d=d):
            sel_copy(j, d).wait_send()
            term_copy(1, j, d).wait_send()
            term_copy(0, j, d).wait_send()

    for c in range(SENDS):
        for r in range(1, kvh_count):
            gq_copy(c, r).wait()
    for copy in stores:
        copy.wait()


def finish(ctx_count, distances, att, gq, own, terms, sel, att_hbm, gq_hbm, gk_hbm, gv_hbm, total, sem):
    me = lax.axis_index("ctx")
    stores = [
        pltpu.make_async_copy(src, dst, sem.at[i])
        for i, (src, dst) in enumerate(
            [(att, att_hbm), (gq, gq_hbm), (total.at[0], gk_hbm), (total.at[1], gv_hbm)]
        )
    ]
    stores[0].start()
    stores[1].start()
    for i in range(2):
        total[i, 0:KBLK] = own[i]
        total[i, KBLK : 2 * KBLK] = jnp.zeros((KBLK, HD), jnp.float32)
    for j, d in enumerate(distances):

        @pl.when(me + d < ctx_count)
        def _(j=j, d=d):
            where = jnp.broadcast_to(sel[j, :, j + 1 : j + 2], (KBLK, HD)) - 2 * me
            for i in range(2):
                term = terms[i, j].astype(jnp.float32)
                total[i, 0:KBLK] += jnp.where(where == 0, term, 0.0)
                total[i, KBLK : 2 * KBLK] += jnp.where(where == 1, term, 0.0)

    stores[2].start()
    stores[3].start()
    for copy in stores:
        copy.wait()


def solution(mesh):
    ctx_count = mesh.shape["ctx"]
    kvh_count = mesh.shape["kvh"]
    distances = [1 << j for j in range(SLOTS - 1) if 1 << j < ctx_count]
    far = len(distances)
    slots = 1 + far

    def on_device(queries, keys, values, upstream, selected, counts):
        tokens, width = queries.shape
        key_rows = keys.shape[0]
        assert tokens == QBLK and key_rows == 2 * KBLK and selected.shape[0] == 1
        bf16, f32 = jnp.bfloat16, jnp.float32
        dma = pltpu.SemaphoreType.DMA
        smem = pl.BlockSpec(memory_space=pltpu.SMEM)
        hbm = pl.BlockSpec(memory_space=pltpu.HBM)
        vmem = pl.BlockSpec(memory_space=pltpu.VMEM)
        anywhere = pl.BlockSpec(memory_space=pl.ANY)
        result = [
            jax.ShapeDtypeStruct((tokens, width), bf16),
            jax.ShapeDtypeStruct((tokens // kvh_count, width * kvh_count), bf16),
        ]
        grad = jax.ShapeDtypeStruct((key_rows, HD), f32)
        parts = pl.pallas_call(
            functools.partial(kernel, ctx_count, kvh_count, distances),
            out_shape=result
            + [
                jax.ShapeDtypeStruct((2, KBLK, HD), f32),
                jax.ShapeDtypeStruct((2, far, KBLK, HD), bf16),
                jax.ShapeDtypeStruct((far, 1, SLOTS), jnp.int32),
            ],
            in_specs=[smem] + [hbm] * 5,
            out_specs=[anywhere] * 5,
            scratch_shapes=[
                pltpu.VMEM((tokens, width), bf16),
                pltpu.VMEM((tokens, width), bf16),
                pltpu.VMEM((key_rows, HD), bf16),
                pltpu.VMEM((key_rows, HD), bf16),
                pltpu.VMEM((far, 2 * KBLK, HD), bf16),
                pltpu.VMEM((far, 2 * KBLK, HD), bf16),
                pltpu.VMEM((far, 1, SLOTS), jnp.int32),
                pltpu.VMEM((slots * KBLK, HD), bf16),
                pltpu.VMEM((slots * KBLK, HD), bf16),
                pltpu.VMEM((slots * KBLK, GROUP * tokens), f32),
                pltpu.VMEM((slots * KBLK, GROUP * tokens), bf16),
                pltpu.VMEM((slots * KBLK, GROUP * tokens), bf16),
                pltpu.VMEM((tokens, width), bf16),
                pltpu.VMEM((tokens, width), bf16),
                pltpu.VMEM((2, KBLK, HD), f32),
                pltpu.VMEM((2, far, KBLK, HD), bf16),
                dma((4,)),
                dma((4,)),
                dma((far,)),
                dma((far,)),
                dma((far,)),
                dma((far,)),
                dma((2, far)),
                dma((2, far)),
                dma((SENDS, kvh_count - 1)),
                dma((SENDS, kvh_count - 1)),
            ],
            compiler_params=pltpu.CompilerParams(
                collective_id=0, has_side_effects=True, vmem_limit_bytes=32 * 1024 * 1024
            ),
        )(
            counts,
            *[
                pltpu.with_memory_space_constraint(x, pltpu.HBM)
                for x in (selected, queries, keys, values, upstream)
            ],
        )
        return pl.pallas_call(
            functools.partial(finish, ctx_count, distances),
            out_shape=result + [grad, grad],
            in_specs=[anywhere, anywhere, vmem, vmem, vmem],
            out_specs=[hbm] * 4,
            scratch_shapes=[pltpu.VMEM((2, key_rows, HD), f32), dma((4,))],
            compiler_params=pltpu.CompilerParams(vmem_limit_bytes=4 * 1024 * 1024),
        )(*parts)

    placed = (
        P("ctx", "kvh"),
        P("ctx", "kvh"),
        P("ctx", "kvh"),
        P("ctx", "kvh"),
        P("ctx", None),
        P("ctx"),
    )
    return jax.shard_map(
        on_device,
        mesh=mesh,
        in_specs=placed,
        out_specs=(P("ctx", "kvh"), P(("ctx", "kvh"), None), P("ctx", "kvh"), P("ctx", "kvh")),
        check_vma=False,
    )
```

```python
import functools
import math

import jax
import jax.numpy as jnp
from jax import lax
from jax.experimental import pallas as pl
from jax.experimental.pallas import tpu as pltpu
from jax.sharding import PartitionSpec as P

HD = 128
GROUP = 8
KBLK = 64
QBLK = 128
SLOTS = 8
PAIR = 2

MESH = pl.DeviceIdType.MESH
LOG2E = math.log2(math.e)
NN = (((1,), (0,)), ((), ()))


def dot(a, b, dims):
    return lax.dot_general(a, b, dims, preferred_element_type=jnp.float32)


def kernel(
    ctx_count,
    kvh_count,
    distances,
    cnt_ref,
    sel_hbm,
    q_hbm,
    k_hbm,
    v_hbm,
    u_hbm,
    att_out,
    gq_out,
    own_out,
    terms_in,
    sel_in,
    sel_ref,
    q_v,
    u_v,
    q_t,
    u_t,
    k_own,
    v_own,
    k_in,
    v_in,
    sel_out,
    keys,
    vals,
    prob,
    prob_half,
    grad_scores,
    att_v,
    gq_v,
    own,
    terms_out,
    load_sem,
    store_sem,
    kv_send,
    kv_recv,
    sel_send,
    sel_recv,
    term_send,
    term_recv,
    gq_send,
    gq_recv,
):
    score_scale = 1.0 / math.sqrt(HD)
    bf16, f32 = jnp.bfloat16, jnp.float32
    me = lax.axis_index("ctx")
    head = lax.axis_index("kvh")
    slots = 1 + len(distances)
    part = QBLK // kvh_count
    width = GROUP * HD
    chunks = GROUP // PAIR
    lanes = PAIR * QBLK

    loads = [
        pltpu.make_async_copy(src, dst, load_sem.at[i])
        for i, (src, dst) in enumerate(
            [
                (sel_hbm, sel_ref),
                (k_hbm, k_own),
                (v_hbm, v_own),
                (q_hbm, q_v),
                (u_hbm, u_v),
            ]
        )
    ]
    for copy in loads:
        copy.start()

    barrier = pltpu.get_barrier_semaphore()
    for r in range(1, kvh_count):
        peer = lax.rem(head + r, kvh_count)
        pl.semaphore_signal(barrier, inc=1, device_id={"kvh": peer}, device_id_type=MESH)
    for d in distances:

        @pl.when(me + d < ctx_count)
        def _():
            pl.semaphore_signal(barrier, inc=1, device_id={"ctx": me + d}, device_id_type=MESH)

        @pl.when(me - d >= 0)
        def _():
            pl.semaphore_signal(barrier, inc=1, device_id={"ctx": me - d}, device_id_type=MESH)

    for copy in loads[:3]:
        copy.wait()
    for j, d in enumerate(distances):
        sel_out[j] = jnp.full((8, HD), sel_ref[0, j + 1] - 2 * (me - d), jnp.int32)

    partners = kvh_count - 1
    for d in distances:
        partners += 1 - (me + d) // ctx_count + (me - d + ctx_count) // ctx_count
    pl.semaphore_wait(barrier, partners)

    def remote(src, dst, send, recv, **where):
        return pltpu.make_async_remote_copy(
            src_ref=src, dst_ref=dst, send_sem=send, recv_sem=recv,
            device_id=where, device_id_type=MESH,
        )

    def k_copy(j, d):
        return remote(k_own, k_in.at[j], kv_send.at[0, j], kv_recv.at[0, j], ctx=me + d)

    def v_copy(j, d):
        return remote(v_own, v_in.at[j], kv_send.at[1, j], kv_recv.at[1, j], ctx=me + d)

    def sel_copy(j, d):
        return remote(sel_out.at[j], sel_in.at[j], sel_send.at[j], sel_recv.at[j], ctx=me - d)

    def term_copy(i, j, d):
        return remote(
            terms_out.at[i, j], terms_in.at[i, j], term_send.at[i, j], term_recv.at[i, j], ctx=me - d
        )

    def gq_copy(c, r):
        cols = PAIR * HD
        peer = lax.rem(head + r, kvh_count)
        return remote(
            gq_v.at[pl.ds(pl.multiple_of(peer * part, part), part), pl.ds(c * cols, cols)],
            gq_out.at[:, pl.ds(pl.multiple_of(head * width + c * cols, cols), cols)],
            gq_send.at[c, r - 1],
            gq_recv.at[c, r - 1],
            kvh=peer,
        )

    by_far = list(enumerate(distances))[::-1]
    for make in (k_copy, v_copy):
        for j, d in by_far:

            @pl.when(me + d < ctx_count)
            def _(make=make, j=j, d=d):
                make(j, d).start()

    for j, d in by_far:

        @pl.when(me - d >= 0)
        def _(j=j, d=d):
            sel_copy(j, d).start()

    for copy in loads[3:]:
        copy.wait()
    for h in range(GROUP):
        at = slice(h * HD, (h + 1) * HD)
        q_t[:, at] = q_v[:, at].astype(f32).T.astype(bf16)
        u_t[:, at] = u_v[:, at].astype(f32).T.astype(bf16)

    count = cnt_ref[0]

    def receive(make, own_rows, arrived, chosen):
        chosen[0:KBLK] = own_rows[0:KBLK]
        for j, d in enumerate(distances):

            @pl.when(me - d >= 0)
            def _(j=j, d=d):
                make(j, d).wait_recv()

            live = jnp.full((KBLK, HD), count > j + 1)
            upper = jnp.full((KBLK, HD), sel_ref[0, j + 1] - 2 * (me - d) > 0)
            lo = arrived[j, 0:KBLK].astype(f32)
            hi = arrived[j, KBLK : 2 * KBLK].astype(f32)
            rows = jnp.where(live, jnp.where(upper, hi, lo), 0.0)
            chosen[(j + 1) * KBLK : (j + 2) * KBLK] = rows.astype(bf16)
        return chosen[...]

    def send_terms(i, term):
        own[i] = term[0:KBLK]
        for j, d in by_far:
            terms_out[i, j] = term[(j + 1) * KBLK : (j + 2) * KBLK].astype(bf16)

            @pl.when(me - d >= 0)
            def _(j=j, d=d):
                term_copy(i, j, d).start()

    def by_rows(ref):
        return jnp.concatenate([ref[:, h * HD : (h + 1) * HD] for h in range(GROUP)], axis=0)

    k_all = receive(k_copy, k_own, k_in, keys)
    key_at = lax.broadcasted_iota(jnp.int32, (KBLK, lanes), 0)
    query_at = lax.rem(lax.broadcasted_iota(jnp.int32, (KBLK, lanes), 1), QBLK)
    causal = key_at <= query_at
    hidden = [jnp.full((KBLK, lanes), count <= j) for j in range(1, slots)]
    for c in range(chunks):
        at = slice(c * lanes, (c + 1) * lanes)
        s = dot(k_all, q_t[:, at], NN)
        s = jnp.concatenate(
            [jnp.where(causal, s[0:KBLK], -1e30)]
            + [
                jnp.where(hidden[j - 1], -1e30, s[j * KBLK : (j + 1) * KBLK])
                for j in range(1, slots)
            ],
            axis=0,
        )
        peak = jnp.max(s, axis=0, keepdims=True)
        e = jnp.exp2((s - peak) * (score_scale * LOG2E))
        p = e * (1.0 / jnp.sum(e, axis=0, keepdims=True))
        prob[:, at] = p
        prob_half[:, at] = p.astype(bf16)
    send_terms(1, dot(prob_half[...], by_rows(u_v), NN))

    v_all = receive(v_copy, v_own, v_in, vals)
    for c in range(chunks):
        at = slice(c * lanes, (c + 1) * lanes)
        dp = dot(v_all, u_t[:, at], NN)
        p = prob[:, at]
        row_term = jnp.sum(p * dp, axis=0, keepdims=True)
        ds = (p * (dp - row_term)).astype(bf16)
        grad_scores[:, at] = ds
    send_terms(0, dot(grad_scores[...], by_rows(q_v), NN) * score_scale)

    k_t = k_all.astype(f32).T.astype(bf16)
    for c in range(chunks):
        at = slice(c * lanes, (c + 1) * lanes)
        gq_c = dot(k_t, grad_scores[:, at], NN) * score_scale
        for i in range(PAIR):
            h = c * PAIR + i
            gq_v[:, h * HD : (h + 1) * HD] = gq_c[:, i * QBLK : (i + 1) * QBLK].T.astype(bf16)
        for r in range(1, kvh_count):
            gq_copy(c, r).start()

    v_t = v_all.astype(f32).T.astype(bf16)
    for c in range(chunks):
        at = slice(c * lanes, (c + 1) * lanes)
        att_c = dot(v_t, prob_half[:, at], NN)
        for i in range(PAIR):
            h = c * PAIR + i
            att_v[:, h * HD : (h + 1) * HD] = att_c[:, i * QBLK : (i + 1) * QBLK].T.astype(bf16)

    stores = [
        pltpu.make_async_copy(
            gq_v.at[pl.ds(pl.multiple_of(head * part, part), part), :],
            gq_out.at[:, pl.ds(pl.multiple_of(head * width, width), width)],
            store_sem.at[0],
        ),
        pltpu.make_async_copy(own, own_out, store_sem.at[1]),
        pltpu.make_async_copy(att_v, att_out, store_sem.at[2]),
    ]
    for copy in stores:
        copy.start()

    for j, d in enumerate(distances):

        @pl.when(me + d < ctx_count)
        def _(j=j, d=d):
            k_copy(j, d).wait_send()
            v_copy(j, d).wait_send()
            sel_copy(j, d).wait_recv()
            term_copy(1, j, d).wait_recv()
            term_copy(0, j, d).wait_recv()

        @pl.when(me - d >= 0)
        def _(j=j, d=d):
            sel_copy(j, d).wait_send()
            term_copy(1, j, d).wait_send()
            term_copy(0, j, d).wait_send()

    for c in range(chunks):
        for r in range(1, kvh_count):
            gq_copy(c, r).wait()
    for copy in stores:
        copy.wait()


def finish(ctx_count, distances, att, gq, own, terms, sel, att_hbm, gq_hbm, gk_hbm, gv_hbm, total, sem):
    me = lax.axis_index("ctx")
    stores = [
        pltpu.make_async_copy(src, dst, sem.at[i])
        for i, (src, dst) in enumerate(
            [(att, att_hbm), (gq, gq_hbm), (total.at[0], gk_hbm), (total.at[1], gv_hbm)]
        )
    ]
    stores[0].start()
    stores[1].start()
    for i in range(2):
        total[i, 0:KBLK] = own[i]
        total[i, KBLK : 2 * KBLK] = jnp.zeros((KBLK, HD), jnp.float32)
    for j, d in enumerate(distances):

        @pl.when(me + d < ctx_count)
        def _(j=j, d=d):
            where = jnp.broadcast_to(sel[j, 0:1], (KBLK, HD))
            for i in range(2):
                term = terms[i, j].astype(jnp.float32)
                total[i, 0:KBLK] += jnp.where(where == 0, term, 0.0)
                total[i, KBLK : 2 * KBLK] += jnp.where(where == 1, term, 0.0)

    stores[2].start()
    stores[3].start()
    for copy in stores:
        copy.wait()


def solution(mesh):
    ctx_count = mesh.shape["ctx"]
    kvh_count = mesh.shape["kvh"]
    distances = [1 << j for j in range(SLOTS - 1) if 1 << j < ctx_count]
    far = len(distances)
    slots = 1 + far

    def on_device(queries, keys, values, upstream, selected, counts):
        tokens, width = queries.shape
        key_rows = keys.shape[0]
        assert tokens == QBLK and key_rows == 2 * KBLK and selected.shape[0] == 1
        chunks = GROUP // PAIR
        bf16, f32 = jnp.bfloat16, jnp.float32
        dma = pltpu.SemaphoreType.DMA
        smem = pl.BlockSpec(memory_space=pltpu.SMEM)
        hbm = pl.BlockSpec(memory_space=pltpu.HBM)
        vmem = pl.BlockSpec(memory_space=pltpu.VMEM)
        anywhere = pl.BlockSpec(memory_space=pl.ANY)
        result = [
            jax.ShapeDtypeStruct((tokens, width), bf16),
            jax.ShapeDtypeStruct((tokens // kvh_count, width * kvh_count), bf16),
        ]
        grad = jax.ShapeDtypeStruct((key_rows, HD), f32)
        parts = pl.pallas_call(
            functools.partial(kernel, ctx_count, kvh_count, distances),
            out_shape=result
            + [
                jax.ShapeDtypeStruct((2, KBLK, HD), f32),
                jax.ShapeDtypeStruct((2, far, KBLK, HD), bf16),
                jax.ShapeDtypeStruct((far, 8, HD), jnp.int32),
            ],
            in_specs=[smem] + [hbm] * 5,
            out_specs=[anywhere] * 5,
            scratch_shapes=[
                pltpu.SMEM((1, SLOTS), jnp.int32),
                pltpu.VMEM((tokens, width), bf16),
                pltpu.VMEM((tokens, width), bf16),
                pltpu.VMEM((HD, GROUP * tokens), bf16),
                pltpu.VMEM((HD, GROUP * tokens), bf16),
                pltpu.VMEM((key_rows, HD), bf16),
                pltpu.VMEM((key_rows, HD), bf16),
                pltpu.VMEM((far, key_rows, HD), bf16),
                pltpu.VMEM((far, key_rows, HD), bf16),
                pltpu.VMEM((far, 8, HD), jnp.int32),
                pltpu.VMEM((slots * KBLK, HD), bf16),
                pltpu.VMEM((slots * KBLK, HD), bf16),
                pltpu.VMEM((slots * KBLK, GROUP * tokens), f32),
                pltpu.VMEM((slots * KBLK, GROUP * tokens), bf16),
                pltpu.VMEM((slots * KBLK, GROUP * tokens), bf16),
                pltpu.VMEM((tokens, width), bf16),
                pltpu.VMEM((tokens, width), bf16),
                pltpu.VMEM((2, KBLK, HD), f32),
                pltpu.VMEM((2, far, KBLK, HD), bf16),
                dma((5,)),
                dma((3,)),
                dma((2, far)),
                dma((2, far)),
                dma((far,)),
                dma((far,)),
                dma((2, far)),
                dma((2, far)),
                dma((chunks, kvh_count - 1)),
                dma((chunks, kvh_count - 1)),
            ],
            compiler_params=pltpu.CompilerParams(
                collective_id=0, has_side_effects=True, vmem_limit_bytes=32 * 1024 * 1024
            ),
        )(
            counts,
            *[
                pltpu.with_memory_space_constraint(x, pltpu.HBM)
                for x in (selected, queries, keys, values, upstream)
            ],
        )
        return pl.pallas_call(
            functools.partial(finish, ctx_count, distances),
            out_shape=result + [grad, grad],
            in_specs=[anywhere, anywhere, vmem, vmem, vmem],
            out_specs=[hbm] * 4,
            scratch_shapes=[pltpu.VMEM((2, key_rows, HD), f32), dma((4,))],
            compiler_params=pltpu.CompilerParams(vmem_limit_bytes=4 * 1024 * 1024),
        )(*parts)

    placed = (
        P("ctx", "kvh"),
        P("ctx", "kvh"),
        P("ctx", "kvh"),
        P("ctx", "kvh"),
        P("ctx", None),
        P("ctx"),
    )
    return jax.shard_map(
        on_device,
        mesh=mesh,
        in_specs=placed,
        out_specs=(P("ctx", "kvh"), P(("ctx", "kvh"), None), P("ctx", "kvh"), P("ctx", "kvh")),
        check_vma=False,
    )
```
